256 devices in a mesh: gx: 64 (over y, z_lo, x), gy: 4 (over z_hi, core).
Axes of the slice: x: 4, y: 4, z: 8 (z_hi: 2, z_lo: 4; z = z_hi * 4 + z_lo), core: 2. Of those that a mesh axis runs over, the one named last changes fastest.
Arguments:
- tracers: float32 [768, 256, 2, 128], P('gx', 'gy'), may hold values from -6 to 6
- weights: float32 [768, 256, 48], P('gx', 'gy'), may hold values from 0 to 0.5
- offsets: int32 [768, 256, 4], P('gx', 'gy'), may hold values from -2 to 1
- owner: int32 [2, 64], replicated, may hold values from 0 to 63, as said below
- codes: int32 [2, 64], replicated, may hold values from 0 to 3
Outputs:
- updated: float32 [768, 256, 2, 128], P('gx', 'gy')
The draws below stay inside these ranges and needn't reach their ends.
Inputs may be any that keep to these rules, and one draw needn't show every extreme that they name: owner[0, b] names the column block whose first three rows are glued below block b, owner[1, b] the one whose last three rows are glued above it; each row of owner is a permutation of the 64 blocks, so every block's edge rows are glued to exactly one block on each side. `codes`: bit 0 reverses the glued rows along the columns, bit 1 reverses their order.
All inputs are finite; a program needn't handle non-finite values.
Results may differ from the reference program's by a relative error of at most 0.0003.
Values sent between devices are 32-bit elements; how exact they have to be, the bound alone decides.
A program may use at most 128 MiB of HBM per device.

```python
import jax
import jax.numpy as jnp
from jax import lax

CX = 12
LEV = 2
Q = 128
BLOCKS = 64
NX = 768
NY = 256
N_GX = 64


def draw_owner(key, part):
    lower_perm = jax.random.permutation(jax.random.fold_in(key, 11), BLOCKS).astype(jnp.int32)
    upper_perm = jax.random.permutation(jax.random.fold_in(key, 23), BLOCKS).astype(jnp.int32)
    return jnp.stack([lower_perm, upper_perm], axis=0)


def plant(array, own_key, smallest, largest):
    spot = [jax.random.randint(jax.random.fold_in(own_key, axis), (), 0, length) for axis, length in enumerate(array.shape)]
    widest = array.shape.index(max(array.shape))
    neighbour = spot[:widest] + [(spot[widest] + 1) % array.shape[widest]] + spot[widest + 1:]
    return array.at[tuple(spot)].set(smallest).at[tuple(neighbour)].set(largest)


def steps_of(key, shape, pieces, least, top_value):
    def one(axis_at, parts):
        steps = jax.random.uniform(jax.random.fold_in(jax.random.fold_in(key, 6), axis_at), (parts,), jnp.float32, least / len(pieces), top_value / len(pieces))
        return jnp.repeat(jnp.exp(steps), shape[axis_at] // parts).reshape((-1,) + (1,) * (len(shape) - axis_at - 1))

    factor_of = one(*pieces[0])
    for cut in pieces[1:]:
        factor_of = factor_of * one(*cut)
    return factor_of


def centred(rng, dims, scale, reach, cuts=(), kind=jnp.bfloat16):
    gain = steps_of(rng, dims, cuts, -0.22, 0.18) if cuts else 1.0
    array = jax.random.normal(rng, dims, jnp.float32) * scale * gain
    return jnp.minimum(jnp.maximum(array, -reach), reach).astype(kind)


def setup_inputs(seed: int = 0) -> dict:
    keys = jax.random.split(jax.random.key(seed), 6)
    return {
        "tracers": centred(keys[0], (NX, NY, LEV, Q), 1.0, 6.0, ((0, 64), (1, 4)), jnp.float32),
        "weights": jnp.clip(0.5 * jax.random.uniform(keys[1], (NX, NY, LEV * 24), jnp.float32) ** steps_of(keys[1], (NX, NY, LEV * 24), ((0, 64), (1, 4)), -0.2, 0.2), 0.0, 0.5),
        "offsets": plant(jax.random.randint(keys[2], (NX, NY, LEV * 2), -2, 2), jax.random.fold_in(keys[2], 1), -2, 1).astype(jnp.int32),
        "owner": draw_owner(jax.random.fold_in(keys[5], 71), 0),
        "codes": plant(jax.random.randint(keys[4], (2, BLOCKS), 0, 4), jax.random.fold_in(keys[4], 1), 0, 3).astype(jnp.int32),
    }


def moment_list(extended):
    centre = extended[1:-1, 1:-1]
    east_side = extended[2:, 1:-1]
    west_side = extended[:-2, 1:-1]
    north_side = extended[1:-1, 2:]
    south_side = extended[1:-1, :-2]
    slope_east = 0.5 * (east_side - west_side)
    slope_north = 0.5 * (north_side - south_side)
    curve_east = 0.5 * (east_side - 2.0 * centre + west_side)
    curve_north = 0.5 * (north_side - 2.0 * centre + south_side)
    twist_both = 0.25 * (extended[2:, 2:] - extended[2:, :-2] - extended[:-2, 2:] + extended[:-2, :-2])
    return [centre, slope_east, slope_north, curve_east, curve_north, twist_both]


def remap_block(extended, weights, offsets):
    cols_out, rows_out = weights.shape[0], weights.shape[1]
    levels = offsets.shape[2] // 2
    tracer_count = extended.shape[3]
    moments = moment_list(extended)
    cols_mom, rows_mom = moments[0].shape[0], moments[0].shape[1]
    grid_cols = jnp.arange(cols_out, dtype=jnp.int32)[:, None]
    grid_rows = jnp.arange(rows_out, dtype=jnp.int32)[None, :]
    results = []
    for level_index in range(levels):
        moment_rows = jnp.stack([moment[:, :, level_index, :] for moment in moments], axis=2)
        moment_rows = moment_rows.reshape(cols_mom * rows_mom, 6 * tracer_count)
        summed = jnp.zeros((cols_out * rows_out, tracer_count), jnp.float32)
        for piece_index in range(4):
            step_col = piece_index // 2
            step_row = piece_index % 2
            source_col = grid_cols + offsets[:, :, 2 * level_index] + (step_col + 2)
            source_row = grid_rows + offsets[:, :, 2 * level_index + 1] + (step_row + 2)
            flat_index = (source_col * rows_mom + source_row).reshape(-1).astype(jnp.int32)
            gathered = jnp.take(moment_rows, flat_index, axis=0).reshape(-1, 6, tracer_count)
            first_weight = level_index * 24 + piece_index * 6
            piece_weights = weights[:, :, first_weight:first_weight + 6].reshape(-1, 6)
            summed = summed + jnp.einsum("ck,ckq->cq", piece_weights, gathered, precision=lax.Precision.HIGHEST)
        results.append(summed.reshape(cols_out, rows_out, tracer_count))
    return jnp.stack(results, axis=2)


def glued_strip(tracers, owner, codes, side_index, block_index):
    source_block = owner[side_index, block_index]
    code_value = codes[side_index, block_index]
    strip_cols = (source_block * CX - 3 + jnp.arange(CX + 6, dtype=jnp.int32)) % NX
    first_row = 0 if side_index == 0 else NY - 3
    strip_rows = jnp.take(tracers[:, first_row:first_row + 3], strip_cols.astype(jnp.int32), axis=0)
    strip_rows = jnp.where(code_value % 2 == 1, strip_rows[::-1], strip_rows)
    return jnp.where((code_value // 2) % 2 == 1, strip_rows[:, ::-1], strip_rows)


def reference(tracers, weights, offsets, owner, codes):
    def one_block(block_index):
        block_cols = (block_index * CX - 3 + jnp.arange(CX + 6, dtype=jnp.int32)) % NX
        middle = jnp.take(tracers, block_cols.astype(jnp.int32), axis=0)
        below = glued_strip(tracers, owner, codes, 0, block_index)
        above = glued_strip(tracers, owner, codes, 1, block_index)
        extended = jnp.concatenate([below, middle, above], axis=1)
        first_col = (block_index * CX).astype(jnp.int32)
        block_weights = lax.dynamic_slice_in_dim(weights, first_col, CX, 0)
        block_offsets = lax.dynamic_slice_in_dim(offsets, first_col, CX, 0)
        return remap_block(extended, block_weights, block_offsets)

    blocks = lax.map(one_block, jnp.arange(N_GX, dtype=jnp.int32))
    return blocks.reshape(NX, NY, LEV, Q)
```

```python
import functools

import jax
import jax.numpy as jnp
from jax import lax
from jax.experimental import pallas as pl
from jax.experimental.pallas import tpu as pltpu
from jax.sharding import PartitionSpec as P

MESH = pl.DeviceIdType.MESH
F32, BF16 = jnp.float32, jnp.bfloat16
COLS, ROWS, HALO = 12, 64, 3
EXT = COLS + 2 * HALO
PAIRS = 2 * HALO
LINES = 2 * ROWS
TOP = LINES + PAIRS
TALL = 144
BANDS = 8
GROUPS = ((3, 6), (0, 3), (9, 3))


def stencil_rows():
    rows = []
    for i in range(4):
        for j in range(8):
            rows.append([0.0] * 24)
    for a in range(2):
        for e in range(2):
            for k, taps in enumerate((
                {(0, 0): 1.0},
                {(1, 0): 0.5, (-1, 0): -0.5},
                {(0, 1): 0.5, (0, -1): -0.5},
                {(1, 0): 0.5, (0, 0): -1.0, (-1, 0): 0.5},
                {(0, 1): 0.5, (0, 0): -1.0, (0, -1): 0.5},
                {(1, 1): 0.25, (1, -1): -0.25, (-1, 1): -0.25, (-1, -1): 0.25},
            )):
                for (u, v), value in taps.items():
                    rows[(a + 1 + u) * 8 + e + 1 + v][6 * (2 * a + e) + k] += value
    return rows


def halves(value):
    high = value.astype(BF16)
    return high, (value - high.astype(F32)).astype(BF16)


def matrices(weights, offsets, taps, flat, tall, mats):
    for x in range(COLS):
        w = weights[x]
        flat[:, 128 * x : 128 * x + 128] = jnp.concatenate([w[:24], w[24:]], axis=1)
    tall[...] = jnp.zeros_like(tall)
    coefs = jnp.dot(taps[...], flat[...], precision=lax.Precision.HIGHEST, preferred_element_type=F32)
    row = lax.broadcasted_iota(jnp.int32, (8, 128), 0)
    inner = lax.broadcasted_iota(jnp.int32, (8, 128), 1) % 8
    for first, count in GROUPS:
        for xl in range(count):
            x = first + xl
            o = offsets[x]
            cols = jnp.concatenate([o[0:1], o[2:3]], axis=1) + 2
            lines = jnp.concatenate([o[1:2], o[3:4]], axis=1) + 2
            shift = jnp.broadcast_to(lines, (8, 128)) + inner
            steps = jnp.broadcast_to(cols, (8, 128))
            pick = (row - shift) & 7
            in_low = row >= shift
            in_high = (row < shift) & (shift <= row + 8)
            zero = jnp.zeros((8, 128), F32)
            low, high = [], []
            for i in range(4):
                turned = jnp.take_along_axis(coefs[8 * i : 8 * i + 8, 128 * x : 128 * x + 128], pick, axis=0)
                low.append(jnp.where(in_low, turned, zero))
                high.append(jnp.where(in_high, turned, zero))
            odd, two = (steps & 1) == 1, steps >= 2
            for part, pieces in enumerate((low, high)):
                pieces = [zero] + pieces + [zero]
                once = [jnp.where(odd, pieces[d], pieces[d + 1]) for d in range(5)]
                once = [zero, zero] + once + [zero, zero]
                for d in range(7):
                    at = 16 * (xl + d) + 8 * part
                    tall[x, at : at + 8, :] = jnp.where(two, once[d], once[d + 2])
    for x in range(COLS):
        mats[:, :, 8 * x : 8 * x + 8, :] = jnp.transpose(tall[x]).reshape(2, BANDS, 8, 256)


def remap(bands, groups, field, mats, out):
    def band(step, carry):
        b = bands[0] + step * (bands[1] - bands[0] if len(bands) > 1 else 1)
        base = pl.multiple_of(16 * b, 16)
        for first, count in groups:
            depth = 16 * (count + PAIRS)
            for level in range(2):
                mat = mats[level, b, 8 * first : 8 * (first + count), :depth]
                mat_high, mat_low = halves(mat)
                cells = field[first : first + count + PAIRS, pl.ds(base + level, 16, 2), :]
                cell_high, cell_low = halves(cells.reshape(depth, 128))
                both = jnp.dot(mat_high, jnp.concatenate([cell_high, cell_low], axis=1), preferred_element_type=F32)
                result = both[:, :128] + both[:, 128:] + jnp.dot(mat_low, cell_high, preferred_element_type=F32)
                for xl in range(count):
                    out[first + xl, pl.ds(base + level, 8, 2), :] = result[8 * xl : 8 * xl + 8]
        return carry

    lax.fori_loop(0, len(bands), band, 0, unroll=True)


def kernel(
    owner, codes, tracers, weights_in, offsets_in, taps, out,
    field, weights, offsets, flat, tall, mats, gathered, chosen, landed,
    in_sem, side_send, side_recv, row_send, row_recv, all_send, all_recv, last_send, last_recv,
):
    gx, gy = lax.axis_index("gx"), lax.axis_index("gy")
    y, z, x = gx // 16, (gx // 4) % 4, gx % 4
    east, west = (gx + 1) % 64, (gx + 63) % 64
    edge = (gy == 0) | (gy == 3)
    me = y * 4 + x

    def peer(step):
        p = (me + step) % 16
        return (p // 4) * 16 + z * 4 + p % 4

    def along(step):
        return y * 16 + ((z + step) % 4) * 4 + x

    loads = [
        pltpu.make_async_copy(weights_in, weights, in_sem.at[0]),
        pltpu.make_async_copy(offsets_in, offsets, in_sem.at[1]),
        pltpu.make_async_copy(tracers, field.at[HALO : HALO + COLS, PAIRS:TOP, :], in_sem.at[2]),
    ]
    for load in loads:
        load.start()

    barrier = pltpu.get_barrier_semaphore()

    def greet(to_x, to_y):
        pl.semaphore_signal(barrier, inc=1, device_id=(to_x, to_y), device_id_type=MESH)

    greet(east, gy)
    greet(west, gy)

    @pl.when(gy > 0)
    def _():
        for to in (west, gx, east):
            greet(to, gy - 1)

    @pl.when(gy < 3)
    def _():
        for to in (west, gx, east):
            greet(to, gy + 1)

    @pl.when(edge)
    def _():
        for step in range(1, 16):
            greet(peer(step), gy)
        for step in range(1, 4):
            greet(along(step), gy)
        pl.semaphore_wait(barrier, 23)

    @pl.when(jnp.logical_not(edge))
    def _():
        pl.semaphore_wait(barrier, 8)

    def send(source, target, send_sem, recv_sem, to):
        return pltpu.make_async_remote_copy(
            src_ref=source, dst_ref=target, send_sem=send_sem, recv_sem=recv_sem, device_id=to, device_id_type=MESH
        )

    edge_at = jnp.where(gy == 0, 0, LINES - PAIRS)
    strip = tracers.at[:, pl.ds(edge_at, PAIRS), :]

    def gather_copy(step):
        return send(
            strip, gathered.at[me, :, 0:PAIRS, :], all_send.at[step], all_recv.at[me], (peer(step), gy)
        )

    def gather_wait(step):
        p = (me + step) % 16
        return send(
            strip, gathered.at[p, :, 0:PAIRS, :], all_send.at[step], all_recv.at[p], (peer(step), gy)
        )

    own_strip = pltpu.make_async_copy(strip, gathered.at[me, :, 0:PAIRS, :], in_sem.at[3])

    @pl.when(edge)
    def _():
        own_strip.start()
        for step in range(1, 16):
            gather_copy(step).start()

    def row_copies(up):
        source = pl.ds(LINES - PAIRS, PAIRS) if up else pl.ds(0, PAIRS)
        target = pl.ds(0, PAIRS) if up else pl.ds(TOP, PAIRS)
        to = gy + 1 if up else gy - 1
        base = 0 if up else 3
        return [
            send(tracers.at[:, source, :], field.at[HALO : HALO + COLS, target, :],
                 row_send.at[base], row_recv.at[base], (gx, to)),
            send(tracers.at[0:HALO, source, :], field.at[HALO + COLS : EXT, target, :],
                 row_send.at[base + 1], row_recv.at[base + 1], (west, to)),
            send(tracers.at[COLS - HALO : COLS, source, :], field.at[0:HALO, target, :],
                 row_send.at[base + 2], row_recv.at[base + 2], (east, to)),
        ]

    @pl.when(gy < 3)
    def _():
        for copy in row_copies(True):
            copy.start()

    @pl.when(gy > 0)
    def _():
        for copy in row_copies(False):
            copy.start()

    to_west = send(tracers.at[0:HALO], field.at[HALO + COLS : EXT, PAIRS:TOP, :], side_send.at[0], side_recv.at[0], (west, gy))
    to_east = send(tracers.at[COLS - HALO : COLS], field.at[0:HALO, PAIRS:TOP, :], side_send.at[1], side_recv.at[1], (east, gy))
    to_west.start()
    to_east.start()

    for c in range(EXT):
        field[c, TOP + PAIRS : TALL, :] = jnp.zeros((TALL - TOP - PAIRS, 128), F32)

    loads[0].wait()
    loads[1].wait()
    matrices(weights, offsets, taps, flat, tall, mats)
    loads[2].wait()

    side = jnp.where(gy == 0, 0, 1)

    def index_of(block):
        return (block // 16) * 4 + block % 4

    def last_copy(step):
        return send(
            chosen.at[step, :, 0:PAIRS, :], landed.at[z, :, 0:PAIRS, :],
            last_send.at[step], last_recv.at[z], (along(step), gy),
        )

    def last_wait(step):
        p = (z + step) % 4
        return send(
            chosen.at[step, :, 0:PAIRS, :], landed.at[p, :, 0:PAIRS, :],
            last_send.at[step], last_recv.at[p], (along(step), gy),
        )

    @pl.when(edge)
    def _():
        own_strip.wait()
        for step in range(1, 16):
            gather_wait(step).wait_recv()
        for step in (1, 2, 3, 0):
            block = owner[side, along(step)]
            mid = gathered[index_of(block), :, 0:PAIRS, :]
            left = gathered[index_of((block + 63) % 64), COLS - HALO : COLS, 0:PAIRS, :]
            right = gathered[index_of((block + 1) % 64), 0:HALO, 0:PAIRS, :]
            if step:
                chosen[step, 0:HALO, 0:PAIRS, :] = left
                chosen[step, HALO : HALO + COLS, 0:PAIRS, :] = mid
                chosen[step, HALO + COLS : EXT, 0:PAIRS, :] = right
                last_copy(step).start()
            else:
                landed[z, 0:HALO, 0:PAIRS, :] = left
                landed[z, HALO : HALO + COLS, 0:PAIRS, :] = mid
                landed[z, HALO + COLS : EXT, 0:PAIRS, :] = right

    remap((1, 2, 3, 4, 5, 6), GROUPS[:1], field, mats, out)
    to_west.wait()
    to_east.wait()
    remap((1, 2, 3, 4, 5, 6), GROUPS[1:], field, mats, out)

    @pl.when(gy > 0)
    def _():
        for copy in row_copies(True):
            copy.wait_recv()

    @pl.when(gy < 3)
    def _():
        for copy in row_copies(False):
            copy.wait_recv()

    @pl.when(edge)
    def _():
        for step in range(1, 4):
            last_wait(step).wait_recv()
        block = owner[side, gx]
        code = codes[side, gx]
        turn, flip = code % 2, (code // 2) % 2

        def level_of(b):
            return (b // 4) % 4

        zs = (level_of((block + 63) % 64), level_of(block), level_of((block + 1) % 64))
        for u in range(EXT):
            v = jnp.where(turn == 1, EXT - 1 - u, u)
            west_z, east_z = (zs[0], zs[2])
            if u < HALO:
                part = jnp.where(turn == 1, east_z, west_z)
            elif u < HALO + COLS:
                part = zs[1]
            else:
                part = jnp.where(turn == 1, west_z, east_z)
            piece = landed[part, v, 0:PAIRS, :]
            back = jnp.concatenate([piece[4:6], piece[2:4], piece[0:2]], axis=0)
            piece = jnp.where(flip == 1, back, piece)

            @pl.when(gy == 0)
            def _():
                field[u, 0:PAIRS, :] = piece

            @pl.when(gy == 3)
            def _():
                field[u, TOP : TOP + PAIRS, :] = piece

    remap((0, 7), GROUPS, field, mats, out)

    @pl.when(gy < 3)
    def _():
        for copy in row_copies(True):
            copy.wait_send()

    @pl.when(gy > 0)
    def _():
        for copy in row_copies(False):
            copy.wait_send()

    @pl.when(edge)
    def _():
        for step in range(1, 16):
            gather_copy(step).wait_send()
        for step in range(1, 4):
            last_copy(step).wait_send()


def on_device(tracers, weights, offsets, owner, codes):
    lines = tracers.reshape(COLS, LINES, 128)
    taps = jnp.array(stencil_rows(), F32)
    any_space = pl.BlockSpec(memory_space=pl.ANY)
    smem = pl.BlockSpec(memory_space=pltpu.SMEM)
    vmem = pl.BlockSpec(memory_space=pltpu.VMEM)
    dma = pltpu.SemaphoreType.DMA
    result = pl.pallas_call(
        kernel,
        out_shape=jax.ShapeDtypeStruct((COLS, LINES, 128), F32),
        in_specs=[smem, smem, any_space, any_space, any_space, vmem],
        out_specs=vmem,
        scratch_shapes=[
            pltpu.VMEM((EXT, TALL, 128), F32),
            pltpu.VMEM((COLS, 48, ROWS), F32),
            pltpu.VMEM((COLS, 4, ROWS), jnp.int32),
            pltpu.VMEM((24, 128 * COLS), F32),
            pltpu.VMEM((COLS, 256, 128), F32),
            pltpu.VMEM((2, BANDS, 8 * COLS, 256), F32),
            pltpu.VMEM((16, COLS, 8, 128), F32),
            pltpu.VMEM((4, EXT, 8, 128), F32),
            pltpu.VMEM((4, EXT, 8, 128), F32),
            dma((4,)), dma((2,)), dma((2,)), dma((6,)), dma((6,)), dma((16,)), dma((16,)), dma((4,)), dma((4,)),
        ],
        compiler_params=pltpu.CompilerParams(
            collective_id=0, has_side_effects=True, vmem_limit_bytes=40 * 1024 * 1024
        ),
    )(owner, codes, lines, jnp.transpose(weights, (0, 2, 1)), jnp.transpose(offsets, (0, 2, 1)), taps)
    return result.reshape(COLS, ROWS, 2, 128)


def solution(mesh):
    in_specs = (P("gx", "gy", None, None), P("gx", "gy", None), P("gx", "gy", None), P(), P())
    return jax.shard_map(
        on_device, mesh=mesh, in_specs=in_specs, out_specs=P("gx", "gy", None, None), check_vma=False
    )
```

```python
import functools

import jax
import jax.numpy as jnp
from jax import lax
from jax.experimental import pallas as pl
from jax.experimental.pallas import tpu as pltpu
from jax.sharding import PartitionSpec as P

MESH = pl.DeviceIdType.MESH
F32, BF16 = jnp.float32, jnp.bfloat16
COLS, ROWS, HALO = 12, 64, 3
EXT = COLS + 2 * HALO
PAIRS = 2 * HALO
LINES = 2 * ROWS
TOP = LINES + PAIRS
TALL = 144
BANDS = 8
GROUPS = ((3, 6), (0, 3), (9, 3))


def stencil():
    shape = (32, 24)
    tap, term = (lax.broadcasted_iota(jnp.int32, shape, dim) for dim in range(2))
    piece, kind = term // 6, term % 6
    u, v = tap // 8 - piece // 2 - 1, tap % 8 - piece % 2 - 1
    near_u, near_v = jnp.abs(u) <= 1, jnp.abs(v) <= 1
    on_u, on_v = near_u & (v == 0), near_v & (u == 0)
    uf, vf = u.astype(F32), v.astype(F32)
    zero = jnp.zeros(shape, F32)
    centre = jnp.where((u == 0) & (v == 0), 1.0, zero)
    value = jnp.where(kind == 0, centre, zero)
    value = jnp.where((kind == 1) & on_u, 0.5 * uf, value)
    value = jnp.where((kind == 2) & on_v, 0.5 * vf, value)
    value = jnp.where((kind == 3) & on_u, 0.5 - 1.5 * centre, value)
    value = jnp.where((kind == 4) & on_v, 0.5 - 1.5 * centre, value)
    return jnp.where((kind == 5) & near_u & near_v, 0.25 * uf * vf, value)


def halves(value):
    high = value.astype(BF16)
    return high, (value - high.astype(F32)).astype(BF16)


def matrices(weights, offsets, flat, tall, mats):
    for x in range(COLS):
        w = weights[x]
        flat[:, 128 * x : 128 * x + 128] = jnp.concatenate([w[:24], w[24:]], axis=1)
    tall[...] = jnp.zeros_like(tall)
    coefs = jnp.dot(stencil(), flat[...], precision=lax.Precision.HIGHEST, preferred_element_type=F32)
    row = lax.broadcasted_iota(jnp.int32, (8, 128), 0)
    inner = lax.broadcasted_iota(jnp.int32, (8, 128), 1) % 8
    for first, count in GROUPS:
        for xl in range(count):
            x = first + xl
            o = offsets[x]
            cols = jnp.concatenate([o[0:1], o[2:3]], axis=1) + 2
            lines = jnp.concatenate([o[1:2], o[3:4]], axis=1) + 2
            shift = jnp.broadcast_to(lines, (8, 128)) + inner
            steps = jnp.broadcast_to(cols, (8, 128))
            pick = (row - shift) & 7
            in_low = row >= shift
            in_high = (row < shift) & (shift <= row + 8)
            zero = jnp.zeros((8, 128), F32)
            low, high = [], []
            for i in range(4):
                turned = jnp.take_along_axis(coefs[8 * i : 8 * i + 8, 128 * x : 128 * x + 128], pick, axis=0)
                low.append(jnp.where(in_low, turned, zero))
                high.append(jnp.where(in_high, turned, zero))
            odd, two = (steps & 1) == 1, steps >= 2
            for part, pieces in enumerate((low, high)):
                pieces = [zero] + pieces + [zero]
                once = [jnp.where(odd, pieces[d], pieces[d + 1]) for d in range(5)]
                once = [zero, zero] + once + [zero, zero]
                for d in range(7):
                    at = 16 * (xl + d) + 8 * part
                    tall[x, at : at + 8, :] = jnp.where(two, once[d], once[d + 2])
    for x in range(COLS):
        mats[:, :, 8 * x : 8 * x + 8, :] = jnp.transpose(tall[x]).reshape(2, BANDS, 8, 256)


def remap(bands, groups, field, mats, out):
    def band(step, carry):
        b = bands[0] + step * (bands[1] - bands[0] if len(bands) > 1 else 1)
        base = pl.multiple_of(16 * b, 16)
        for first, count in groups:
            depth = 16 * (count + PAIRS)
            for level in range(2):
                mat = mats[level, b, 8 * first : 8 * (first + count), :depth]
                mat_high, mat_low = halves(mat)
                cells = field[first : first + count + PAIRS, pl.ds(base + level, 16, 2), :]
                cell_high, cell_low = halves(cells.reshape(depth, 128))
                both = jnp.dot(mat_high, jnp.concatenate([cell_high, cell_low], axis=1), preferred_element_type=F32)
                result = both[:, :128] + both[:, 128:] + jnp.dot(mat_low, cell_high, preferred_element_type=F32)
                for xl in range(count):
                    out[first + xl, pl.ds(base + level, 8, 2), :] = result[8 * xl : 8 * xl + 8]
        return carry

    lax.fori_loop(0, len(bands), band, 0, unroll=True)


def kernel(
    owner_in, codes_in, tracers, weights_in, offsets_in, out,
    owner, codes, field, weights, offsets, flat, tall, mats, gathered, chosen, landed,
    in_sem, side_send, side_recv, row_send, row_recv, all_send, all_recv, last_send, last_recv,
):
    gx, gy = lax.axis_index("gx"), lax.axis_index("gy")
    y, z, x = gx // 16, (gx // 4) % 4, gx % 4
    east, west = (gx + 1) % 64, (gx + 63) % 64
    edge = (gy == 0) | (gy == 3)
    me = y * 4 + x

    def peer(step):
        p = (me + step) % 16
        return (p // 4) * 16 + z * 4 + p % 4

    def along(step):
        return y * 16 + ((z + step) % 4) * 4 + x

    loads = [
        pltpu.make_async_copy(weights_in, weights, in_sem.at[0]),
        pltpu.make_async_copy(offsets_in, offsets, in_sem.at[1]),
        pltpu.make_async_copy(owner_in, owner, in_sem.at[4]),
        pltpu.make_async_copy(codes_in, codes, in_sem.at[5]),
        pltpu.make_async_copy(tracers, field.at[HALO : HALO + COLS, PAIRS:TOP, :], in_sem.at[2]),
    ]
    for load in loads:
        load.start()

    barrier = pltpu.get_barrier_semaphore()

    def greet(to_x, to_y):
        pl.semaphore_signal(barrier, inc=1, device_id=(to_x, to_y), device_id_type=MESH)

    greet(east, gy)
    greet(west, gy)

    @pl.when(gy > 0)
    def _():
        for to in (west, gx, east):
            greet(to, gy - 1)

    @pl.when(gy < 3)
    def _():
        for to in (west, gx, east):
            greet(to, gy + 1)

    @pl.when(edge)
    def _():
        for step in range(1, 16):
            greet(peer(step), gy)
        for step in range(1, 4):
            greet(along(step), gy)
        pl.semaphore_wait(barrier, 23)

    @pl.when(jnp.logical_not(edge))
    def _():
        pl.semaphore_wait(barrier, 8)

    def send(source, target, send_sem, recv_sem, to):
        return pltpu.make_async_remote_copy(
            src_ref=source, dst_ref=target, send_sem=send_sem, recv_sem=recv_sem, device_id=to, device_id_type=MESH
        )

    edge_at = jnp.where(gy == 0, 0, LINES - PAIRS)
    strip = tracers.at[:, pl.ds(edge_at, PAIRS), :]

    def gather_copy(step):
        return send(
            strip, gathered.at[me, :, 0:PAIRS, :], all_send.at[step], all_recv.at[me], (peer(step), gy)
        )

    def gather_wait(step):
        p = (me + step) % 16
        return send(
            strip, gathered.at[p, :, 0:PAIRS, :], all_send.at[step], all_recv.at[p], (peer(step), gy)
        )

    own_strip = pltpu.make_async_copy(strip, gathered.at[me, :, 0:PAIRS, :], in_sem.at[3])

    @pl.when(edge)
    def _():
        own_strip.start()
        for step in range(1, 16):
            gather_copy(step).start()

    def row_copies(up):
        source = pl.ds(LINES - PAIRS, PAIRS) if up else pl.ds(0, PAIRS)
        target = pl.ds(0, PAIRS) if up else pl.ds(TOP, PAIRS)
        to = gy + 1 if up else gy - 1
        base = 0 if up else 3
        return [
            send(tracers.at[:, source, :], field.at[HALO : HALO + COLS, target, :],
                 row_send.at[base], row_recv.at[base], (gx, to)),
            send(tracers.at[0:HALO, source, :], field.at[HALO + COLS : EXT, target, :],
                 row_send.at[base + 1], row_recv.at[base + 1], (west, to)),
            send(tracers.at[COLS - HALO : COLS, source, :], field.at[0:HALO, target, :],
                 row_send.at[base + 2], row_recv.at[base + 2], (east, to)),
        ]

    @pl.when(gy < 3)
    def _():
        for copy in row_copies(True):
            copy.start()

    @pl.when(gy > 0)
    def _():
        for copy in row_copies(False):
            copy.start()

    to_west = send(tracers.at[0:HALO], field.at[HALO + COLS : EXT, PAIRS:TOP, :], side_send.at[0], side_recv.at[0], (west, gy))
    to_east = send(tracers.at[COLS - HALO : COLS], field.at[0:HALO, PAIRS:TOP, :], side_send.at[1], side_recv.at[1], (east, gy))
    to_west.start()
    to_east.start()

    for c in range(EXT):
        field[c, TOP + PAIRS : TALL, :] = jnp.zeros((TALL - TOP - PAIRS, 128), F32)

    loads[0].wait()
    loads[1].wait()
    matrices(weights, offsets, flat, tall, mats)
    for load in loads[2:]:
        load.wait()

    side = jnp.where(gy == 0, 0, 1)

    def index_of(block):
        return (block // 16) * 4 + block % 4

    def last_copy(step):
        return send(
            chosen.at[step, :, 0:PAIRS, :], landed.at[z, :, 0:PAIRS, :],
            last_send.at[step], last_recv.at[z], (along(step), gy),
        )

    def last_wait(step):
        p = (z + step) % 4
        return send(
            chosen.at[step, :, 0:PAIRS, :], landed.at[p, :, 0:PAIRS, :],
            last_send.at[step], last_recv.at[p], (along(step), gy),
        )

    @pl.when(edge)
    def _():
        own_strip.wait()
        for step in range(1, 16):
            gather_wait(step).wait_recv()
        for step in (1, 2, 3, 0):
            block = owner[side, along(step)]
            mid = gathered[index_of(block), :, 0:PAIRS, :]
            left = gathered[index_of((block + 63) % 64), COLS - HALO : COLS, 0:PAIRS, :]
            right = gathered[index_of((block + 1) % 64), 0:HALO, 0:PAIRS, :]
            if step:
                chosen[step, 0:HALO, 0:PAIRS, :] = left
                chosen[step, HALO : HALO + COLS, 0:PAIRS, :] = mid
                chosen[step, HALO + COLS : EXT, 0:PAIRS, :] = right
                last_copy(step).start()
            else:
                landed[z, 0:HALO, 0:PAIRS, :] = left
                landed[z, HALO : HALO + COLS, 0:PAIRS, :] = mid
                landed[z, HALO + COLS : EXT, 0:PAIRS, :] = right

    remap((1, 2, 3, 4, 5, 6), GROUPS[:1], field, mats, out)
    to_west.wait()
    to_east.wait()
    remap((1, 2, 3, 4, 5, 6), GROUPS[1:], field, mats, out)

    @pl.when(gy > 0)
    def _():
        for copy in row_copies(True):
            copy.wait_recv()

    @pl.when(gy < 3)
    def _():
        for copy in row_copies(False):
            copy.wait_recv()

    @pl.when(edge)
    def _():
        for step in range(1, 4):
            last_wait(step).wait_recv()
        block = owner[side, gx]
        code = codes[side, gx]
        turn, flip = code % 2, (code // 2) % 2

        def level_of(b):
            return (b // 4) % 4

        zs = (level_of((block + 63) % 64), level_of(block), level_of((block + 1) % 64))
        for u in range(EXT):
            v = jnp.where(turn == 1, EXT - 1 - u, u)
            west_z, east_z = (zs[0], zs[2])
            if u < HALO:
                part = jnp.where(turn == 1, east_z, west_z)
            elif u < HALO + COLS:
                part = zs[1]
            else:
                part = jnp.where(turn == 1, west_z, east_z)
            piece = landed[part, v, 0:PAIRS, :]
            back = jnp.concatenate([piece[4:6], piece[2:4], piece[0:2]], axis=0)
            piece = jnp.where(flip == 1, back, piece)

            @pl.when(gy == 0)
            def _():
                field[u, 0:PAIRS, :] = piece

            @pl.when(gy == 3)
            def _():
                field[u, TOP : TOP + PAIRS, :] = piece

    remap((0, 7), GROUPS, field, mats, out)

    @pl.when(gy < 3)
    def _():
        for copy in row_copies(True):
            copy.wait_send()

    @pl.when(gy > 0)
    def _():
        for copy in row_copies(False):
            copy.wait_send()

    @pl.when(edge)
    def _():
        for step in range(1, 16):
            gather_copy(step).wait_send()
        for step in range(1, 4):
            last_copy(step).wait_send()


def on_device(tracers, weights, offsets, owner, codes):
    lines = tracers.reshape(COLS, LINES, 128)
    hbm = pl.BlockSpec(memory_space=pltpu.HBM)
    vmem = pl.BlockSpec(memory_space=pltpu.VMEM)
    dma = pltpu.SemaphoreType.DMA
    result = pl.pallas_call(
        kernel,
        out_shape=jax.ShapeDtypeStruct((COLS, LINES, 128), F32),
        in_specs=[hbm] * 5,
        out_specs=vmem,
        scratch_shapes=[
            pltpu.SMEM((2, 64), jnp.int32),
            pltpu.SMEM((2, 64), jnp.int32),
            pltpu.VMEM((EXT, TALL, 128), F32),
            pltpu.VMEM((COLS, 48, ROWS), F32),
            pltpu.VMEM((COLS, 4, ROWS), jnp.int32),
            pltpu.VMEM((24, 128 * COLS), F32),
            pltpu.VMEM((COLS, 256, 128), F32),
            pltpu.VMEM((2, BANDS, 8 * COLS, 256), F32),
            pltpu.VMEM((16, COLS, 8, 128), F32),
            pltpu.VMEM((4, EXT, 8, 128), F32),
            pltpu.VMEM((4, EXT, 8, 128), F32),
            dma((6,)), dma((2,)), dma((2,)), dma((6,)), dma((6,)), dma((16,)), dma((16,)), dma((4,)), dma((4,)),
        ],
        compiler_params=pltpu.CompilerParams(
            collective_id=0, has_side_effects=True, vmem_limit_bytes=40 * 1024 * 1024
        ),
    )(*(pltpu.with_memory_space_constraint(a, pltpu.HBM) for a in (owner, codes, lines, jnp.transpose(weights, (0, 2, 1)), jnp.transpose(offsets, (0, 2, 1)))))
    return result.reshape(COLS, ROWS, 2, 128)


def solution(mesh):
    in_specs = (P("gx", "gy", None, None), P("gx", "gy", None), P("gx", "gy", None), P(), P())
    return jax.shard_map(
        on_device, mesh=mesh, in_specs=in_specs, out_specs=P("gx", "gy", None, None), check_vma=False
    )
```

```python
import functools

import jax
import jax.numpy as jnp
from jax import lax
from jax.experimental import pallas as pl
from jax.experimental.pallas import tpu as pltpu
from jax.sharding import PartitionSpec as P

MESH = pl.DeviceIdType.MESH
F32, BF16 = jnp.float32, jnp.bfloat16
COLS, ROWS, HALO = 12, 64, 3
EXT = COLS + 2 * HALO
PAIRS = 2 * HALO
LINES = 2 * ROWS
TOP = LINES + PAIRS
TALL = 144
BANDS = 8
GROUPS = ((3, 6), (0, 3), (9, 3))


def stencil():
    shape = (32, 24)
    tap, term = (lax.broadcasted_iota(jnp.int32, shape, dim) for dim in range(2))
    piece, kind = term // 6, term % 6
    u, v = tap // 8 - piece // 2 - 1, tap % 8 - piece % 2 - 1
    near_u, near_v = jnp.abs(u) <= 1, jnp.abs(v) <= 1
    on_u, on_v = near_u & (v == 0), near_v & (u == 0)
    uf, vf = u.astype(F32), v.astype(F32)
    zero = jnp.zeros(shape, F32)
    centre = jnp.where((u == 0) & (v == 0), 1.0, zero)
    value = jnp.where(kind == 0, centre, zero)
    value = jnp.where((kind == 1) & on_u, 0.5 * uf, value)
    value = jnp.where((kind == 2) & on_v, 0.5 * vf, value)
    value = jnp.where((kind == 3) & on_u, 0.5 - 1.5 * centre, value)
    value = jnp.where((kind == 4) & on_v, 0.5 - 1.5 * centre, value)
    return jnp.where((kind == 5) & near_u & near_v, 0.25 * uf * vf, value)


def halves(value):
    high = value.astype(BF16)
    return high, (value - high.astype(F32)).astype(BF16)


def matrices(weights, offsets, flat, tall, mats):
    for x in range(COLS):
        w = weights[x]
        flat[:, 128 * x : 128 * x + 128] = jnp.concatenate([w[:24], w[24:]], axis=1)
    tall[...] = jnp.zeros_like(tall)
    coefs = jnp.dot(stencil(), flat[...], precision=lax.Precision.HIGHEST, preferred_element_type=F32)
    row = lax.broadcasted_iota(jnp.int32, (8, 128), 0)
    inner = lax.broadcasted_iota(jnp.int32, (8, 128), 1) % 8
    for first, count in GROUPS:
        for xl in range(count):
            x = first + xl
            o = offsets[x]
            cols = jnp.concatenate([o[0:1], o[2:3]], axis=1) + 2
            lines = jnp.concatenate([o[1:2], o[3:4]], axis=1) + 2
            shift = jnp.broadcast_to(lines, (8, 128)) + inner
            steps = jnp.broadcast_to(cols, (8, 128))
            pick = (row - shift) & 7
            in_low = row >= shift
            in_high = (row < shift) & (shift <= row + 8)
            zero = jnp.zeros((8, 128), F32)
            low, high = [], []
            for i in range(4):
                turned = jnp.take_along_axis(coefs[8 * i : 8 * i + 8, 128 * x : 128 * x + 128], pick, axis=0)
                low.append(jnp.where(in_low, turned, zero))
                high.append(jnp.where(in_high, turned, zero))
            odd, two = (steps & 1) == 1, steps >= 2
            for part, pieces in enumerate((low, high)):
                pieces = [zero] + pieces + [zero]
                once = [jnp.where(odd, pieces[d], pieces[d + 1]) for d in range(5)]
                once = [zero, zero] + once + [zero, zero]
                for d in range(7):
                    at = 16 * (xl + d) + 8 * part
                    tall[x, at : at + 8, :] = jnp.where(two, once[d], once[d + 2])
    for x in range(COLS):
        mats[:, :, 8 * x : 8 * x + 8, :] = jnp.transpose(tall[x]).reshape(2, BANDS, 8, 256)


def remap(bands, groups, field, mats, out):
    for b in bands:
        base = 16 * b if isinstance(b, int) else pl.multiple_of(16 * b, 16)
        for first, count in groups:
            depth = 16 * (count + PAIRS)
            for level in range(2):
                mat = mats[level, b, 8 * first : 8 * (first + count), :depth]
                mat_high, mat_low = halves(mat)
                cells = field[first : first + count + PAIRS, pl.ds(base + level, 16, 2), :]
                cell_high, cell_low = halves(cells.reshape(depth, 128))
                both = jnp.dot(mat_high, jnp.concatenate([cell_high, cell_low], axis=1), preferred_element_type=F32)
                result = both[:, :128] + both[:, 128:] + jnp.dot(mat_low, cell_high, preferred_element_type=F32)
                for xl in range(count):
                    out[first + xl, pl.ds(base + level, 8, 2), :] = result[8 * xl : 8 * xl + 8]


WEST, EAST, UP, DOWN, ALONG_Z, PLANE = 0, 1, 2, 5, 8, 11
LINKS = 26
ORDER = (*range(ALONG_Z, LINKS), *range(ALONG_Z))
STEPS = sorted(((j, i) for j in range(4) for i in range(4) if j + i), key=lambda s: -(s[0] % 2 + s[1] % 2 + 2 * (s[0] // 2 * (s[0] % 2 == 0) + s[1] // 2 * (s[1] % 2 == 0))))
BACK = (1, 0, 5, 7, 6, 2, 4, 3) + (10, 9, 8) + tuple(
    PLANE + STEPS.index((-j % 4, -i % 4)) for j, i in STEPS
)


def rank(gx, gy):
    return (gy >> 1) * 256 + ((gx & 15) << 3) + ((gx >> 4) << 1) + 1 - (gy & 1)


def kernel(
    owner_in, codes_in, tracers, weights_in, offsets_in, out,
    owner, codes, field, weights, offsets, flat, tall, mats, gathered, chosen, landed,
    in_sem, side_send, side_recv, row_send, row_recv, one_send, one_recv, two_send, two_recv,
    ready,
):
    gx, gy = lax.axis_index("gx"), lax.axis_index("gy")
    y, z, x = gx >> 4, (gx >> 2) & 3, gx & 3
    east, west = (gx + 1) & 63, (gx + 63) & 63
    edge = (gy == 0) | (gy == 3)
    half = COLS // 2
    edge_at = jnp.where(gy == 0, 0, LINES - PAIRS)

    loads = [
        pltpu.make_async_copy(weights_in, weights, in_sem.at[0]),
        pltpu.make_async_copy(offsets_in, offsets, in_sem.at[1]),
        pltpu.make_async_copy(owner_in, owner, in_sem.at[4]),
        pltpu.make_async_copy(codes_in, codes, in_sem.at[5]),
        pltpu.make_async_copy(tracers, field.at[HALO : HALO + COLS, PAIRS:TOP, :], in_sem.at[2]),
    ]
    own_strip = pltpu.make_async_copy(
        tracers.at[:, pl.ds(edge_at, PAIRS), :], gathered.at[z, :, 0:PAIRS, :], in_sem.at[3]
    )

    always = gy >= 0
    peers = [(west, gy), (east, gy)]
    exists = [always, always]
    for to, there in ((gy + 1, gy < 3), (gy - 1, gy > 0)):
        peers += [(gx, to), (west, to), (east, to)]
        exists += [there] * 3
    peers += [(16 * y + 4 * ((z + k) & 3) + x, gy) for k in (1, 2, 3)]
    peers += [(16 * ((y + j) & 3) + 4 * z + ((x + i) & 3), gy) for j, i in STEPS]
    exists += [edge] * 18
    mine = rank(gx, gy)
    later = [there & (rank(*to) > mine) for to, there in zip(peers, exists)]
    earlier = [there & (rank(*to) < mine) for to, there in zip(peers, exists)]

    barrier = pltpu.get_barrier_semaphore()
    for r in ORDER:

        @pl.when(later[r])
        def _():
            pl.semaphore_signal(barrier, inc=1, device_id=peers[r], device_id_type=MESH)

    @pl.when(edge)
    def _():
        own_strip.start()

    for load in loads:
        load.start()

    ahead = sum(e.astype(jnp.int32) for e in earlier)

    @pl.when(ahead > 0)
    def _():
        pl.semaphore_wait(barrier, ahead)

    def send(source, target, send_sem, recv_sem, to):
        return pltpu.make_async_remote_copy(
            src_ref=source, dst_ref=target, send_sem=send_sem, recv_sem=recv_sem, device_id=to, device_id_type=MESH
        )

    def side_copy(r):
        if r == WEST:
            source, target = tracers.at[0:HALO], field.at[HALO + COLS : EXT, PAIRS:TOP, :]
        else:
            source, target = tracers.at[COLS - HALO : COLS], field.at[0:HALO, PAIRS:TOP, :]
        return send(source, target, side_send.at[r], side_recv.at[r], peers[r])

    def row_copy(r):
        up = r < DOWN
        lines = pl.ds(LINES - PAIRS, PAIRS) if up else pl.ds(0, PAIRS)
        target = pl.ds(0, PAIRS) if up else pl.ds(TOP, PAIRS)
        which = (r - UP) % 3
        taken, put = (
            (slice(0, COLS), slice(HALO, HALO + COLS)),
            (slice(0, HALO), slice(HALO + COLS, EXT)),
            (slice(COLS - HALO, COLS), slice(0, HALO)),
        )[which]
        return send(
            tracers.at[taken, lines, :], field.at[put, target, :], row_send.at[r - UP], row_recv.at[r - UP], peers[r]
        )

    def one_copy(r):
        k = r - ALONG_Z
        return send(
            tracers.at[:, pl.ds(edge_at, PAIRS), :], gathered.at[z, :, 0:PAIRS, :], one_send.at[k], one_recv.at[z], peers[r]
        )

    def one_wait(r):
        k = r - ALONG_Z
        spot = (z + k + 1) & 3
        place = gathered.at[spot, :, 0:PAIRS, :]
        return send(place, place, one_send.at[k], one_recv.at[spot], peers[r])

    def two_copy(r):
        k = r - PLANE
        return send(
            chosen.at[k, :, 0:PAIRS, :], landed.at[y, x, :, 0:PAIRS, :], two_send.at[k], two_recv.at[y, x], peers[r]
        )

    def two_wait(r):
        k = r - PLANE
        j, i = STEPS[k]
        there = (y + j) & 3, (x + i) & 3
        return send(
            chosen.at[k, :, 0:PAIRS, :], landed.at[*there, :, 0:PAIRS, :], two_send.at[k], two_recv.at[*there], peers[r]
        )

    def copy_of(r):
        return side_copy(r) if r < UP else row_copy(r) if r < ALONG_Z else one_copy(r)

    def start_earlier(links):
        for r in links:

            @pl.when(earlier[r])
            def _():
                copy_of(r).start()

    def start_later(links, allowed):
        for r in links:

            @pl.when(later[r] & allowed(r))
            def _():
                pl.semaphore_wait(ready.at[r], 1)
                copy_of(r).start()

    wraps_west, wraps_east = (z == 0) & (x == 0), (z == 3) & (x == 3)

    def far(r):
        wrap = wraps_west if r in (WEST, UP + 1, DOWN + 1) else wraps_east if r in (EAST, UP + 2, DOWN + 2) else gy < 0
        return wrap | ((gy == 1) if UP <= r < DOWN else (gy == 2) if DOWN <= r < ALONG_Z else gy < 0)

    def near(r):
        return jnp.logical_not(far(r))

    rows, sides, plane = range(UP, ALONG_Z), (WEST, EAST), range(PLANE, LINKS)
    tower = range(ALONG_Z, PLANE)
    not_edge = jnp.logical_not(edge)

    def start_sides(who):
        for r in sides:

            @pl.when(who & earlier[r])
            def _():
                copy_of(r).start()

        start_later(sides, lambda r: who & near(r))

    start_earlier(tower)
    for r in ORDER:

        @pl.when(earlier[r])
        def _():
            pl.semaphore_signal(ready.at[BACK[r]], inc=1, device_id=peers[r], device_id_type=MESH)

    start_earlier(rows)
    start_sides(always)
    start_later(rows, near)
    start_later(tower, lambda r: always)

    for c in range(EXT):
        field[c, TOP + PAIRS : TALL, :] = jnp.zeros((TALL - TOP - PAIRS, 128), F32)

    loads[0].wait()
    loads[1].wait()
    matrices(weights, offsets, flat, tall, mats)
    for load in loads[2:]:
        load.wait()

    side = jnp.where(gy == 0, 0, 1)

    @pl.when(edge)
    def _():
        own_strip.wait()
        for r in tower:
            one_wait(r).wait_recv()
        for r in (*plane, None):
            target = gx if r is None else peers[r][0]
            block = owner[side, target]
            parts = [
                gathered[(from_block >> 2) & 3, cols, 0:PAIRS, :]
                for from_block, cols in (
                    ((block + 63) & 63, slice(COLS - HALO, COLS)),
                    (block, slice(0, COLS)),
                    ((block + 1) & 63, slice(0, HALO)),
                )
            ]
            for part, cols in zip(parts, (slice(0, HALO), slice(HALO, HALO + COLS), slice(HALO + COLS, EXT))):
                if r is None:
                    landed[y, x, cols, 0:PAIRS, :] = part
                else:
                    chosen[r - PLANE, cols, 0:PAIRS, :] = part
            if r is not None:

                @pl.when(later[r])
                def _():
                    pl.semaphore_wait(ready.at[r], 1)

                two_copy(r).start()

    remap((1, 2, 3, 4, 5, 6), GROUPS[:1], field, mats, out)

    start_later(rows, far)
    start_later(sides, far)

    for r in sides:
        side_copy(r).wait()
    remap((1, 2, 3, 4, 5, 6), GROUPS[1:], field, mats, out)

    @pl.when(gy > 0)
    def _():
        for r in range(UP, DOWN):
            row_copy(r).wait_recv()
        remap((0,), GROUPS, field, mats, out)

    @pl.when(gy < 3)
    def _():
        for r in range(DOWN, ALONG_Z):
            row_copy(r).wait_recv()
        remap((7,), GROUPS, field, mats, out)

    @pl.when(edge)
    def _():
        for r in plane:
            two_wait(r).wait_recv()
        block = owner[side, gx]
        code = codes[side, gx]
        turn, flip = code & 1, (code >> 1) & 1
        before, after = (block + 63) & 63, (block + 1) & 63
        first, last = jnp.where(turn == 1, after, before), jnp.where(turn == 1, before, after)
        for u in range(EXT):
            v = jnp.where(turn == 1, EXT - 1 - u, u)
            part = first if u < HALO else block if u < HALO + COLS else last
            piece = landed[part >> 4, part & 3, v, 0:PAIRS, :]
            back = jnp.concatenate([piece[4:6], piece[2:4], piece[0:2]], axis=0)
            piece = jnp.where(flip == 1, back, piece)

            @pl.when(gy == 0)
            def _():
                field[u, 0:PAIRS, :] = piece

            @pl.when(gy == 3)
            def _():
                field[u, TOP : TOP + PAIRS, :] = piece

        remap((jnp.where(gy == 0, 0, BANDS - 1),), GROUPS, field, mats, out)
        for r in tower:
            one_copy(r).wait_send()
        for r in plane:
            two_copy(r).wait_send()

    @pl.when(gy < 3)
    def _():
        for r in range(UP, DOWN):
            row_copy(r).wait_send()

    @pl.when(gy > 0)
    def _():
        for r in range(DOWN, ALONG_Z):
            row_copy(r).wait_send()


def on_device(tracers, weights, offsets, owner, codes):
    lines = tracers.reshape(COLS, LINES, 128)
    hbm = pl.BlockSpec(memory_space=pltpu.HBM)
    vmem = pl.BlockSpec(memory_space=pltpu.VMEM)
    dma = pltpu.SemaphoreType.DMA
    result = pl.pallas_call(
        kernel,
        out_shape=jax.ShapeDtypeStruct((COLS, LINES, 128), F32),
        in_specs=[hbm] * 5,
        out_specs=vmem,
        scratch_shapes=[
            pltpu.SMEM((2, 64), jnp.int32),
            pltpu.SMEM((2, 64), jnp.int32),
            pltpu.VMEM((EXT, TALL, 128), F32),
            pltpu.VMEM((COLS, 48, ROWS), F32),
            pltpu.VMEM((COLS, 4, ROWS), jnp.int32),
            pltpu.VMEM((24, 128 * COLS), F32),
            pltpu.VMEM((COLS, 256, 128), F32),
            pltpu.VMEM((2, BANDS, 8 * COLS, 256), F32),
            pltpu.VMEM((4, COLS, 8, 128), F32),
            pltpu.VMEM((15, EXT, 8, 128), F32),
            pltpu.VMEM((4, 4, EXT, 8, 128), F32),
            dma((6,)), dma((2,)), dma((2,)), dma((6,)), dma((6,)), dma((3,)), dma((4,)), dma((15,)), dma((4, 4)), pltpu.SemaphoreType.REGULAR((LINKS,)),
        ],
        compiler_params=pltpu.CompilerParams(
            collective_id=0, has_side_effects=True, vmem_limit_bytes=40 * 1024 * 1024
        ),
    )(*(pltpu.with_memory_space_constraint(a, pltpu.HBM) for a in (owner, codes, lines, jnp.transpose(weights, (0, 2, 1)), jnp.transpose(offsets, (0, 2, 1)))))
    return result.reshape(COLS, ROWS, 2, 128)


def solution(mesh):
    in_specs = (P("gx", "gy", None, None), P("gx", "gy", None), P("gx", "gy", None), P(), P())
    return jax.shard_map(
        on_device, mesh=mesh, in_specs=in_specs, out_specs=P("gx", "gy", None, None), check_vma=False
    )
```

```python
import functools

import jax
import jax.numpy as jnp
from jax import lax
from jax.experimental import pallas as pl
from jax.experimental.pallas import tpu as pltpu
from jax.sharding import PartitionSpec as P

MESH = pl.DeviceIdType.MESH
F32, BF16 = jnp.float32, jnp.bfloat16
COLS, ROWS, HALO = 12, 64, 3
EXT = COLS + 2 * HALO
PAIRS = 2 * HALO
LINES = 2 * ROWS
TOP = LINES + PAIRS
TALL = 144
BANDS = 8
GROUPS = ((3, 6), (0, 3), (9, 3))


def stencil():
    shape = (32, 24)
    tap, term = (lax.broadcasted_iota(jnp.int32, shape, dim) for dim in range(2))
    piece, kind = term // 6, term % 6
    u, v = tap // 8 - piece // 2 - 1, tap % 8 - piece % 2 - 1
    near_u, near_v = jnp.abs(u) <= 1, jnp.abs(v) <= 1
    on_u, on_v = near_u & (v == 0), near_v & (u == 0)
    uf, vf = u.astype(F32), v.astype(F32)
    zero = jnp.zeros(shape, F32)
    centre = jnp.where((u == 0) & (v == 0), 1.0, zero)
    value = jnp.where(kind == 0, centre, zero)
    value = jnp.where((kind == 1) & on_u, 0.5 * uf, value)
    value = jnp.where((kind == 2) & on_v, 0.5 * vf, value)
    value = jnp.where((kind == 3) & on_u, 0.5 - 1.5 * centre, value)
    value = jnp.where((kind == 4) & on_v, 0.5 - 1.5 * centre, value)
    return jnp.where((kind == 5) & near_u & near_v, 0.25 * uf * vf, value)


def halves(value):
    high = value.astype(BF16)
    return high, (value - high.astype(F32)).astype(BF16)


def matrices(weights, offsets, flat, tall, mats):
    for x in range(COLS):
        w = weights[x]
        flat[:, 128 * x : 128 * x + 128] = jnp.concatenate([w[:24], w[24:]], axis=1)
    tall[...] = jnp.zeros_like(tall)
    coefs = jnp.dot(stencil(), flat[...], precision=lax.Precision.HIGHEST, preferred_element_type=F32)
    row = lax.broadcasted_iota(jnp.int32, (8, 128), 0)
    inner = lax.broadcasted_iota(jnp.int32, (8, 128), 1) % 8
    for first, count in GROUPS:
        for xl in range(count):
            x = first + xl
            o = offsets[x]
            cols = jnp.concatenate([o[0:1], o[2:3]], axis=1) + 2
            lines = jnp.concatenate([o[1:2], o[3:4]], axis=1) + 2
            shift = jnp.broadcast_to(lines, (8, 128)) + inner
            steps = jnp.broadcast_to(cols, (8, 128))
            pick = (row - shift) & 7
            in_low = row >= shift
            in_high = (row < shift) & (shift <= row + 8)
            zero = jnp.zeros((8, 128), F32)
            low, high = [], []
            for i in range(4):
                turned = jnp.take_along_axis(coefs[8 * i : 8 * i + 8, 128 * x : 128 * x + 128], pick, axis=0)
                low.append(jnp.where(in_low, turned, zero))
                high.append(jnp.where(in_high, turned, zero))
            odd, two = (steps & 1) == 1, steps >= 2
            for part, pieces in enumerate((low, high)):
                pieces = [zero] + pieces + [zero]
                once = [jnp.where(odd, pieces[d], pieces[d + 1]) for d in range(5)]
                once = [zero, zero] + once + [zero, zero]
                for d in range(7):
                    at = 16 * (xl + d) + 8 * part
                    tall[x, at : at + 8, :] = jnp.where(two, once[d], once[d + 2])
    for x in range(COLS):
        mats[:, :, 8 * x : 8 * x + 8, :] = jnp.transpose(tall[x]).reshape(2, BANDS, 8, 256)


def remap(bands, groups, field, mats, out):
    for b in bands:
        base = 16 * b if isinstance(b, int) else pl.multiple_of(16 * b, 16)
        for first, count in groups:
            depth = 16 * (count + PAIRS)
            for level in range(2):
                mat = mats[level, b, 8 * first : 8 * (first + count), :depth]
                mat_high, mat_low = halves(mat)
                cells = field[first : first + count + PAIRS, pl.ds(base + level, 16, 2), :]
                cell_high, cell_low = halves(cells.reshape(depth, 128))
                both = jnp.dot(mat_high, jnp.concatenate([cell_high, cell_low], axis=1), preferred_element_type=F32)
                result = both[:, :128] + both[:, 128:] + jnp.dot(mat_low, cell_high, preferred_element_type=F32)
                for xl in range(count):
                    out[first + xl, pl.ds(base + level, 8, 2), :] = result[8 * xl : 8 * xl + 8]


WEST, EAST, UP, DOWN, ALONG_Z, PLANE = 0, 1, 2, 5, 8, 11
VIA, LINKS = 26, 27
ORDER = (*range(ALONG_Z, LINKS), *range(ALONG_Z))
STEPS = sorted(((j, i) for j in range(4) for i in range(4) if j + i), key=lambda s: -(s[0] % 2 + s[1] % 2 + 2 * (s[0] // 2 * (s[0] % 2 == 0) + s[1] // 2 * (s[1] % 2 == 0))))
BACK = (1, 0, 5, 7, 6, 2, 4, 3) + (10, 9, 8) + tuple(
    PLANE + STEPS.index((-j % 4, -i % 4)) for j, i in STEPS
) + (VIA,)


def rank(gx, gy):
    return (gy >> 1) * 256 + ((gx & 15) << 3) + ((gx >> 4) << 1) + 1 - (gy & 1)


def kernel(
    owner_in, codes_in, tracers, weights_in, offsets_in, out,
    owner, codes, field, weights, offsets, flat, tall, mats, gathered, chosen, landed, relay,
    in_sem, side_send, side_recv, row_send, row_recv, one_send, one_recv, two_send, two_recv,
    via_send, via_recv, hand_send, ready,
):
    gx, gy = lax.axis_index("gx"), lax.axis_index("gy")
    y, z, x = gx >> 4, (gx >> 2) & 3, gx & 3
    east, west = (gx + 1) & 63, (gx + 63) & 63
    edge = (gy == 0) | (gy == 3)
    half = COLS // 2
    edge_at = jnp.where(gy == 0, 0, LINES - PAIRS)

    loads = [
        pltpu.make_async_copy(weights_in, weights, in_sem.at[0]),
        pltpu.make_async_copy(offsets_in, offsets, in_sem.at[1]),
        pltpu.make_async_copy(owner_in, owner, in_sem.at[4]),
        pltpu.make_async_copy(codes_in, codes, in_sem.at[5]),
        pltpu.make_async_copy(tracers, field.at[HALO : HALO + COLS, PAIRS:TOP, :], in_sem.at[2]),
    ]
    own_strip = pltpu.make_async_copy(
        tracers.at[:, pl.ds(edge_at, PAIRS), :], gathered.at[z, :, 0:PAIRS, :], in_sem.at[3]
    )

    always = gy >= 0
    peers = [(west, gy), (east, gy)]
    exists = [always, always]
    for to, there in ((gy + 1, gy < 3), (gy - 1, gy > 0)):
        peers += [(gx, to), (west, to), (east, to)]
        exists += [there] * 3
    peers += [(16 * y + 4 * ((z + k) & 3) + x, gy) for k in (1, 2, 3)]
    peers += [(16 * ((y + j) & 3) + 4 * z + ((x + i) & 3), gy) for j, i in STEPS]
    exists += [edge] * 18
    wraps_west, wraps_east = (z == 0) & (x == 0), (z == 3) & (x == 3)
    hands_west, hands_east = edge & (z == 0) & (x == 1), edge & (z == 3) & (x == 2)
    via_to_east, via_to_west = edge & wraps_east, edge & wraps_west
    up_y, down_y = 16 * ((y + 1) & 3), 16 * ((y + 3) & 3)
    via = jnp.where(
        via_to_east, up_y + 1, jnp.where(hands_west, down_y + 15, jnp.where(via_to_west, down_y + 14, up_y))
    )
    peers += [(via, gy)]
    exists += [via_to_east | via_to_west | hands_west | hands_east]
    exists[WEST] = jnp.logical_not(via_to_west)
    exists[EAST] = jnp.logical_not(via_to_east)
    mine = rank(gx, gy)
    later = [there & (rank(*to) > mine) for to, there in zip(peers, exists)]
    earlier = [there & (rank(*to) < mine) for to, there in zip(peers, exists)]

    barrier = pltpu.get_barrier_semaphore()
    for r in ORDER:

        @pl.when(later[r])
        def _():
            pl.semaphore_signal(barrier, inc=1, device_id=peers[r], device_id_type=MESH)

    @pl.when(edge)
    def _():
        own_strip.start()

    for load in loads:
        load.start()

    ahead = sum(e.astype(jnp.int32) for e in earlier)

    @pl.when(ahead > 0)
    def _():
        pl.semaphore_wait(barrier, ahead)

    def send(source, target, send_sem, recv_sem, to):
        return pltpu.make_async_remote_copy(
            src_ref=source, dst_ref=target, send_sem=send_sem, recv_sem=recv_sem, device_id=to, device_id_type=MESH
        )

    def side_copy(r):
        if r == WEST:
            source, target = tracers.at[0:HALO], field.at[HALO + COLS : EXT, PAIRS:TOP, :]
        else:
            source, target = tracers.at[COLS - HALO : COLS], field.at[0:HALO, PAIRS:TOP, :]
        return send(source, target, side_send.at[r], side_recv.at[r], peers[r])

    def row_copy(r):
        up = r < DOWN
        lines = pl.ds(LINES - PAIRS, PAIRS) if up else pl.ds(0, PAIRS)
        target = pl.ds(0, PAIRS) if up else pl.ds(TOP, PAIRS)
        which = (r - UP) % 3
        taken, put = (
            (slice(0, COLS), slice(HALO, HALO + COLS)),
            (slice(0, HALO), slice(HALO + COLS, EXT)),
            (slice(COLS - HALO, COLS), slice(0, HALO)),
        )[which]
        return send(
            tracers.at[taken, lines, :], field.at[put, target, :], row_send.at[r - UP], row_recv.at[r - UP], peers[r]
        )

    def one_copy(r):
        k = r - ALONG_Z
        return send(
            tracers.at[:, pl.ds(edge_at, PAIRS), :], gathered.at[z, :, 0:PAIRS, :], one_send.at[k], one_recv.at[z], peers[r]
        )

    def one_wait(r):
        k = r - ALONG_Z
        spot = (z + k + 1) & 3
        place = gathered.at[spot, :, 0:PAIRS, :]
        return send(place, place, one_send.at[k], one_recv.at[spot], peers[r])

    def two_copy(r):
        k = r - PLANE
        return send(
            chosen.at[k, :, 0:PAIRS, :], landed.at[y, x, :, 0:PAIRS, :], two_send.at[k], two_recv.at[y, x], peers[r]
        )

    def two_wait(r):
        k = r - PLANE
        j, i = STEPS[k]
        there = (y + j) & 3, (x + i) & 3
        return send(
            chosen.at[k, :, 0:PAIRS, :], landed.at[*there, :, 0:PAIRS, :], two_send.at[k], two_recv.at[*there], peers[r]
        )

    def copy_of(r):
        return side_copy(r) if r < UP else row_copy(r) if r < ALONG_Z else one_copy(r)

    def start_earlier(links):
        for r in links:

            @pl.when(earlier[r])
            def _():
                copy_of(r).start()

    def start_later(links, allowed):
        for r in links:

            @pl.when(later[r] & allowed(r))
            def _():
                pl.semaphore_wait(ready.at[r], 1)
                copy_of(r).start()

    def far(r):
        wrap = wraps_west if r in (WEST, UP + 1, DOWN + 1) else wraps_east if r in (EAST, UP + 2, DOWN + 2) else gy < 0
        return wrap | ((gy == 1) if UP <= r < DOWN else (gy == 2) if DOWN <= r < ALONG_Z else gy < 0)

    def near(r):
        return jnp.logical_not(far(r))

    def via_copy(r, c, column):
        return send(tracers.at[column], relay.at[c], via_send.at[c], via_recv.at[c], peers[r])

    def start_via(allowed, r, first):
        @pl.when(allowed)
        def _():
            for c in range(HALO):
                via_copy(r, c, first + c).start()

    def hand_copy(r, c):
        column = c if r == EAST else HALO + COLS + c
        return send(relay.at[c], field.at[column, PAIRS:TOP, :], hand_send.at[c], side_recv.at[r], peers[VIA])

    def hand_on(allowed, r):
        @pl.when(allowed & later[VIA])
        def _():
            pl.semaphore_wait(ready.at[VIA], 1)

        @pl.when(allowed)
        def _():
            for c in range(HALO):
                via_copy(r, c, c).wait_recv()
                hand_copy(r, c).start()

    def hand_wait(allowed, r):
        @pl.when(allowed)
        def _():
            for c in range(HALO):
                hand_copy(r, c).wait_send()

    rows, sides, plane = range(UP, ALONG_Z), (WEST, EAST), range(PLANE, VIA)
    tower = range(ALONG_Z, PLANE)
    not_edge = jnp.logical_not(edge)

    def start_sides(who):
        for r in sides:

            @pl.when(who & earlier[r])
            def _():
                copy_of(r).start()

        start_later(sides, lambda r: who & near(r))

    start_earlier(tower)
    for r in ORDER:

        @pl.when(earlier[r])
        def _():
            pl.semaphore_signal(ready.at[BACK[r]], inc=1, device_id=peers[r], device_id_type=MESH)

    start_earlier(rows)
    start_sides(not_edge)
    start_via(via_to_east, WEST, COLS - HALO)
    start_later(rows, lambda r: near(r) & not_edge)
    start_later(tower, lambda r: always)
    start_sides(edge)
    start_via(via_to_west, EAST, 0)
    start_later(rows, lambda r: near(r) & edge)

    for c in range(EXT):
        field[c, TOP + PAIRS : TALL, :] = jnp.zeros((TALL - TOP - PAIRS, 128), F32)

    loads[0].wait()
    loads[1].wait()
    matrices(weights, offsets, flat, tall, mats)
    for load in loads[2:]:
        load.wait()

    side = jnp.where(gy == 0, 0, 1)

    hand_on(hands_east, EAST)

    @pl.when(edge)
    def _():
        own_strip.wait()
        for r in tower:
            one_wait(r).wait_recv()
        for r in (*plane, None):
            target = gx if r is None else peers[r][0]
            block = owner[side, target]
            before, after = (block + 63) & 63, (block + 1) & 63
            column = gx & 51
            pick = jnp.where((before & 51) == column, before, jnp.where((after & 51) == column, after, block))
            part = gathered[(pick >> 2) & 3, :, 0:PAIRS, :]
            if r is None:
                landed[y, x, :, 0:PAIRS, :] = part
            else:
                chosen[r - PLANE, :, 0:PAIRS, :] = part
            if r is not None:

                @pl.when(later[r])
                def _():
                    pl.semaphore_wait(ready.at[r], 1)

                two_copy(r).start()

    remap((1, 2, 3, 4, 5, 6), GROUPS[:1], field, mats, out)

    hand_on(hands_west, WEST)
    start_later(sides, far)
    start_later(rows, far)

    for r in sides:
        side_copy(r).wait_recv()
    remap((1, 2, 3, 4, 5, 6), GROUPS[1:], field, mats, out)

    @pl.when(gy > 0)
    def _():
        for r in range(UP, DOWN):
            row_copy(r).wait_recv()
        remap((0,), GROUPS, field, mats, out)

    @pl.when(gy < 3)
    def _():
        for r in range(DOWN, ALONG_Z):
            row_copy(r).wait_recv()
        remap((7,), GROUPS, field, mats, out)

    @pl.when(edge)
    def _():
        for r in plane:
            two_wait(r).wait_recv()
        block = owner[side, gx]
        code = codes[side, gx]
        turn, flip = code & 1, (code >> 1) & 1
        before, after = (block + 63) & 63, (block + 1) & 63
        first, last = jnp.where(turn == 1, after, before), jnp.where(turn == 1, before, after)
        for u in range(EXT):
            if u < HALO:
                part, v = first, jnp.where(turn == 1, HALO - 1 - u, COLS - HALO + u)
            elif u < HALO + COLS:
                part, v = block, jnp.where(turn == 1, EXT - HALO - 1 - u, u - HALO)
            else:
                part, v = last, jnp.where(turn == 1, COLS - HALO + EXT - 1 - u, u - HALO - COLS)
            piece = landed[part >> 4, part & 3, v, 0:PAIRS, :]
            back = jnp.concatenate([piece[4:6], piece[2:4], piece[0:2]], axis=0)
            piece = jnp.where(flip == 1, back, piece)

            @pl.when(gy == 0)
            def _():
                field[u, 0:PAIRS, :] = piece

            @pl.when(gy == 3)
            def _():
                field[u, TOP : TOP + PAIRS, :] = piece

        remap((jnp.where(gy == 0, 0, BANDS - 1),), GROUPS, field, mats, out)
        for r in tower:
            one_copy(r).wait_send()
        for r in plane:
            two_copy(r).wait_send()

    for r, skip in ((WEST, via_to_west), (EAST, via_to_east)):

        @pl.when(jnp.logical_not(skip))
        def _():
            side_copy(r).wait_send()

    @pl.when(via_to_west | via_to_east)
    def _():
        for c in range(HALO):
            via_copy(WEST, c, c).wait_send()

    @pl.when(via_to_west & later[VIA])
    def _():
        pl.semaphore_wait(ready.at[VIA], 1)

    hand_wait(hands_west, WEST)
    hand_wait(hands_east, EAST)

    @pl.when(gy < 3)
    def _():
        for r in range(UP, DOWN):
            row_copy(r).wait_send()

    @pl.when(gy > 0)
    def _():
        for r in range(DOWN, ALONG_Z):
            row_copy(r).wait_send()


def on_device(tracers, weights, offsets, owner, codes):
    lines = tracers.reshape(COLS, LINES, 128)
    hbm = pl.BlockSpec(memory_space=pltpu.HBM)
    vmem = pl.BlockSpec(memory_space=pltpu.VMEM)
    dma = pltpu.SemaphoreType.DMA
    result = pl.pallas_call(
        kernel,
        out_shape=jax.ShapeDtypeStruct((COLS, LINES, 128), F32),
        in_specs=[hbm] * 5,
        out_specs=vmem,
        scratch_shapes=[
            pltpu.SMEM((2, 64), jnp.int32),
            pltpu.SMEM((2, 64), jnp.int32),
            pltpu.VMEM((EXT, TALL, 128), F32),
            pltpu.VMEM((COLS, 48, ROWS), F32),
            pltpu.VMEM((COLS, 4, ROWS), jnp.int32),
            pltpu.VMEM((24, 128 * COLS), F32),
            pltpu.VMEM((COLS, 256, 128), F32),
            pltpu.VMEM((2, BANDS, 8 * COLS, 256), F32),
            pltpu.VMEM((4, COLS, 8, 128), F32),
            pltpu.VMEM((15, COLS, 8, 128), F32),
            pltpu.VMEM((4, 4, COLS, 8, 128), F32),
            pltpu.VMEM((HALO, LINES, 128), F32),
            dma((6,)), dma((2,)), dma((2,)), dma((6,)), dma((6,)), dma((3,)), dma((4,)), dma((15,)), dma((4, 4)), dma((3,)), dma((3,)), dma((3,)), pltpu.SemaphoreType.REGULAR((LINKS,)),
        ],
        compiler_params=pltpu.CompilerParams(
            collective_id=0, has_side_effects=True, vmem_limit_bytes=40 * 1024 * 1024
        ),
    )(*(pltpu.with_memory_space_constraint(a, pltpu.HBM) for a in (owner, codes, lines, jnp.transpose(weights, (0, 2, 1)), jnp.transpose(offsets, (0, 2, 1)))))
    return result.reshape(COLS, ROWS, 2, 128)


def solution(mesh):
    in_specs = (P("gx", "gy", None, None), P("gx", "gy", None), P("gx", "gy", None), P(), P())
    return jax.shard_map(
        on_device, mesh=mesh, in_specs=in_specs, out_specs=P("gx", "gy", None, None), check_vma=False
    )
```

```python
import functools

import jax
import jax.numpy as jnp
from jax import lax
from jax.experimental import pallas as pl
from jax.experimental.pallas import tpu as pltpu
from jax.sharding import PartitionSpec as P

MESH = pl.DeviceIdType.MESH
F32, BF16 = jnp.float32, jnp.bfloat16
COLS, ROWS, HALO = 12, 64, 3
EXT = COLS + 2 * HALO
PAIRS = 2 * HALO
LINES = 2 * ROWS
TOP = LINES + PAIRS
TALL = 144
BANDS = 8
GROUPS = ((3, 6), (0, 3), (9, 3))


def stencil():
    shape = (32, 24)
    tap, term = (lax.broadcasted_iota(jnp.int32, shape, dim) for dim in range(2))
    piece, kind = term // 6, term % 6
    u, v = tap // 8 - piece // 2 - 1, tap % 8 - piece % 2 - 1
    near_u, near_v = jnp.abs(u) <= 1, jnp.abs(v) <= 1
    on_u, on_v = near_u & (v == 0), near_v & (u == 0)
    uf, vf = u.astype(F32), v.astype(F32)
    zero = jnp.zeros(shape, F32)
    centre = jnp.where((u == 0) & (v == 0), 1.0, zero)
    value = jnp.where(kind == 0, centre, zero)
    value = jnp.where((kind == 1) & on_u, 0.5 * uf, value)
    value = jnp.where((kind == 2) & on_v, 0.5 * vf, value)
    value = jnp.where((kind == 3) & on_u, 0.5 - 1.5 * centre, value)
    value = jnp.where((kind == 4) & on_v, 0.5 - 1.5 * centre, value)
    return jnp.where((kind == 5) & near_u & near_v, 0.25 * uf * vf, value)


def halves(value):
    high = value.astype(BF16)
    return high, (value - high.astype(F32)).astype(BF16)


def matrices(weights, offsets, flat, tall, mats):
    for x in range(COLS):
        w = weights[x]
        flat[:, 128 * x : 128 * x + 128] = jnp.concatenate([w[:24], w[24:]], axis=1)
    tall[...] = jnp.zeros_like(tall)
    coefs = jnp.dot(stencil(), flat[...], precision=lax.Precision.HIGHEST, preferred_element_type=F32)
    row = lax.broadcasted_iota(jnp.int32, (8, 128), 0)
    inner = lax.broadcasted_iota(jnp.int32, (8, 128), 1) % 8
    for first, count in GROUPS:
        for xl in range(count):
            x = first + xl
            o = offsets[x]
            cols = jnp.concatenate([o[0:1], o[2:3]], axis=1) + 2
            lines = jnp.concatenate([o[1:2], o[3:4]], axis=1) + 2
            shift = jnp.broadcast_to(lines, (8, 128)) + inner
            steps = jnp.broadcast_to(cols, (8, 128))
            pick = (row - shift) & 7
            in_low = row >= shift
            in_high = (row < shift) & (shift <= row + 8)
            zero = jnp.zeros((8, 128), F32)
            low, high = [], []
            for i in range(4):
                turned = jnp.take_along_axis(coefs[8 * i : 8 * i + 8, 128 * x : 128 * x + 128], pick, axis=0)
                low.append(jnp.where(in_low, turned, zero))
                high.append(jnp.where(in_high, turned, zero))
            odd, two = (steps & 1) == 1, steps >= 2
            for part, pieces in enumerate((low, high)):
                pieces = [zero] + pieces + [zero]
                once = [jnp.where(odd, pieces[d], pieces[d + 1]) for d in range(5)]
                once = [zero, zero] + once + [zero, zero]
                for d in range(7):
                    at = 16 * (xl + d) + 8 * part
                    tall[x, at : at + 8, :] = jnp.where(two, once[d], once[d + 2])
    for x in range(COLS):
        mats[:, :, 8 * x : 8 * x + 8, :] = jnp.transpose(tall[x]).reshape(2, BANDS, 8, 256)


def remap(bands, groups, field, mats, out):
    for b in bands:
        base = 16 * b if isinstance(b, int) else pl.multiple_of(16 * b, 16)
        for first, count in groups:
            depth = 16 * (count + PAIRS)
            for level in range(2):
                mat = mats[level, b, 8 * first : 8 * (first + count), :depth]
                mat_high, mat_low = halves(mat)
                cells = field[first : first + count + PAIRS, pl.ds(base + level, 16, 2), :]
                cell_high, cell_low = halves(cells.reshape(depth, 128))
                both = jnp.dot(mat_high, jnp.concatenate([cell_high, cell_low], axis=1), preferred_element_type=F32)
                result = both[:, :128] + both[:, 128:] + jnp.dot(mat_low, cell_high, preferred_element_type=F32)
                for xl in range(count):
                    out[first + xl, pl.ds(base + level, 8, 2), :] = result[8 * xl : 8 * xl + 8]


WEST, EAST, UP, DOWN, ALONG_Z, PLANE = 0, 1, 2, 5, 8, 11
VIA, LINKS = 26, 27
ORDER = (*range(ALONG_Z, LINKS), *range(ALONG_Z))
STEPS = sorted(((j, i) for j in range(4) for i in range(4) if j + i), key=lambda s: -(s[0] % 2 + s[1] % 2 + 2 * (s[0] // 2 * (s[0] % 2 == 0) + s[1] // 2 * (s[1] % 2 == 0))))
BACK = (1, 0, 5, 7, 6, 2, 4, 3) + (10, 9, 8) + tuple(
    PLANE + STEPS.index((-j % 4, -i % 4)) for j, i in STEPS
) + (VIA,)


def rank(gx, gy):
    return (gy >> 1) * 256 + ((gx & 15) << 3) + ((gx >> 4) << 1) + 1 - (gy & 1)


def kernel(
    owner_in, codes_in, tracers, weights_in, offsets_in, out,
    owner, codes, field, weights, offsets, flat, tall, mats, gathered, chosen, landed, relay,
    in_sem, side_send, side_recv, row_send, row_recv, one_send, one_recv, two_send, two_recv,
    via_send, via_recv, hand_send, ready,
):
    gx, gy = lax.axis_index("gx"), lax.axis_index("gy")
    y, z, x = gx >> 4, (gx >> 2) & 3, gx & 3
    east, west = (gx + 1) & 63, (gx + 63) & 63
    edge = (gy == 0) | (gy == 3)
    half = COLS // 2
    edge_at = jnp.where(gy == 0, 0, LINES - PAIRS)

    loads = [
        pltpu.make_async_copy(weights_in, weights, in_sem.at[0]),
        pltpu.make_async_copy(offsets_in, offsets, in_sem.at[1]),
        pltpu.make_async_copy(owner_in, owner, in_sem.at[4]),
        pltpu.make_async_copy(codes_in, codes, in_sem.at[5]),
        pltpu.make_async_copy(tracers, field.at[HALO : HALO + COLS, PAIRS:TOP, :], in_sem.at[2]),
    ]
    own_strip = pltpu.make_async_copy(
        tracers.at[:, pl.ds(edge_at, PAIRS), :], gathered.at[z, :, 0:PAIRS, :], in_sem.at[3]
    )

    always = gy >= 0
    peers = [(west, gy), (east, gy)]
    exists = [always, always]
    for to, there in ((gy + 1, gy < 3), (gy - 1, gy > 0)):
        peers += [(gx, to), (west, to), (east, to)]
        exists += [there] * 3
    peers += [(16 * y + 4 * ((z + k) & 3) + x, gy) for k in (1, 2, 3)]
    peers += [(16 * ((y + j) & 3) + 4 * z + ((x + i) & 3), gy) for j, i in STEPS]
    exists += [edge] * 18
    wraps_west, wraps_east = (z == 0) & (x == 0), (z == 3) & (x == 3)
    hands_west, hands_east = edge & (z == 0) & (x == 1), edge & (z == 3) & (x == 2)
    via_to_east, via_to_west = edge & wraps_east, edge & wraps_west
    up_y, down_y = 16 * ((y + 1) & 3), 16 * ((y + 3) & 3)
    via = jnp.where(
        via_to_east, up_y + 1, jnp.where(hands_west, down_y + 15, jnp.where(via_to_west, down_y + 14, up_y))
    )
    peers += [(via, gy)]
    exists += [via_to_east | via_to_west | hands_west | hands_east]
    exists[WEST] = jnp.logical_not(via_to_west)
    exists[EAST] = jnp.logical_not(via_to_east)
    mine = rank(gx, gy)
    later = [there & (rank(*to) > mine) for to, there in zip(peers, exists)]
    earlier = [there & (rank(*to) < mine) for to, there in zip(peers, exists)]

    barrier = pltpu.get_barrier_semaphore()
    for r in ORDER:

        @pl.when(later[r])
        def _():
            pl.semaphore_signal(barrier, inc=1, device_id=peers[r], device_id_type=MESH)

    @pl.when(edge)
    def _():
        own_strip.start()

    for load in loads:
        load.start()

    ahead = sum(e.astype(jnp.int32) for e in earlier)

    @pl.when(ahead > 0)
    def _():
        pl.semaphore_wait(barrier, ahead)

    def send(source, target, send_sem, recv_sem, to):
        return pltpu.make_async_remote_copy(
            src_ref=source, dst_ref=target, send_sem=send_sem, recv_sem=recv_sem, device_id=to, device_id_type=MESH
        )

    def side_copy(r):
        if r == WEST:
            source, target = tracers.at[0:HALO], field.at[HALO + COLS : EXT, PAIRS:TOP, :]
        else:
            source, target = tracers.at[COLS - HALO : COLS], field.at[0:HALO, PAIRS:TOP, :]
        return send(source, target, side_send.at[r], side_recv.at[r], peers[r])

    def row_copy(r):
        up = r < DOWN
        lines = pl.ds(LINES - PAIRS, PAIRS) if up else pl.ds(0, PAIRS)
        target = pl.ds(0, PAIRS) if up else pl.ds(TOP, PAIRS)
        which = (r - UP) % 3
        taken, put = (
            (slice(0, COLS), slice(HALO, HALO + COLS)),
            (slice(0, HALO), slice(HALO + COLS, EXT)),
            (slice(COLS - HALO, COLS), slice(0, HALO)),
        )[which]
        return send(
            tracers.at[taken, lines, :], field.at[put, target, :], row_send.at[r - UP], row_recv.at[r - UP], peers[r]
        )

    def one_copy(r):
        k = r - ALONG_Z
        return send(
            tracers.at[:, pl.ds(edge_at, PAIRS), :], gathered.at[z, :, 0:PAIRS, :], one_send.at[k], one_recv.at[z], peers[r]
        )

    def one_wait(r):
        k = r - ALONG_Z
        spot = (z + k + 1) & 3
        place = gathered.at[spot, :, 0:PAIRS, :]
        return send(place, place, one_send.at[k], one_recv.at[spot], peers[r])

    def two_copy(r):
        k = r - PLANE
        return send(
            chosen.at[k, :, 0:PAIRS, :], landed.at[y, x, :, 0:PAIRS, :], two_send.at[k], two_recv.at[y, x], peers[r]
        )

    def two_wait(r):
        k = r - PLANE
        j, i = STEPS[k]
        there = (y + j) & 3, (x + i) & 3
        return send(
            chosen.at[k, :, 0:PAIRS, :], landed.at[*there, :, 0:PAIRS, :], two_send.at[k], two_recv.at[*there], peers[r]
        )

    def copy_of(r):
        return side_copy(r) if r < UP else row_copy(r) if r < ALONG_Z else one_copy(r)

    def start_earlier(links):
        for r in links:

            @pl.when(earlier[r])
            def _():
                copy_of(r).start()

    def start_later(links, allowed):
        for r in links:

            @pl.when(later[r] & allowed(r))
            def _():
                pl.semaphore_wait(ready.at[r], 1)
                copy_of(r).start()

    def far(r):
        wrap = wraps_west if r in (WEST, UP + 1, DOWN + 1) else wraps_east if r in (EAST, UP + 2, DOWN + 2) else gy < 0
        return wrap | ((gy == 1) if UP <= r < DOWN else (gy == 2) if DOWN <= r < ALONG_Z else gy < 0)

    def near(r):
        return jnp.logical_not(far(r))

    def via_copy(r, c, column):
        return send(tracers.at[column], relay.at[c], via_send.at[c], via_recv.at[c], peers[r])

    def start_via(allowed, r, first):
        @pl.when(allowed)
        def _():
            for c in range(HALO):
                via_copy(r, c, first + c).start()

    def hand_copy(r, c):
        column = c if r == EAST else HALO + COLS + c
        return send(relay.at[c], field.at[column, PAIRS:TOP, :], hand_send.at[c], side_recv.at[r], peers[VIA])

    def hand_on(allowed, r):
        @pl.when(allowed & later[VIA])
        def _():
            pl.semaphore_wait(ready.at[VIA], 1)

        @pl.when(allowed)
        def _():
            for c in range(HALO):
                via_copy(r, c, c).wait_recv()
                hand_copy(r, c).start()

    def hand_wait(allowed, r):
        @pl.when(allowed)
        def _():
            for c in range(HALO):
                hand_copy(r, c).wait_send()

    rows, sides, plane = range(UP, ALONG_Z), (WEST, EAST), range(PLANE, VIA)
    tower = range(ALONG_Z, PLANE)
    not_edge = jnp.logical_not(edge)

    def start_sides(who):
        start_later((EAST,), lambda r: who & near(r) & (x == 3))
        for r in sides:

            @pl.when(who & earlier[r])
            def _():
                copy_of(r).start()

        start_later(sides, lambda r: who & near(r) & ((x < 3) if r == EAST else always))

    start_earlier(tower)
    for r in ORDER:

        @pl.when(earlier[r])
        def _():
            pl.semaphore_signal(ready.at[BACK[r]], inc=1, device_id=peers[r], device_id_type=MESH)

    start_earlier(rows)
    start_sides(not_edge)
    start_via(via_to_east, WEST, COLS - HALO)
    start_later(rows, lambda r: near(r) & not_edge)
    start_later(tower, lambda r: always)
    start_sides(edge)
    start_via(via_to_west, EAST, 0)
    start_later(rows, lambda r: near(r) & edge)

    for c in range(EXT):
        field[c, TOP + PAIRS : TALL, :] = jnp.zeros((TALL - TOP - PAIRS, 128), F32)

    loads[0].wait()
    loads[1].wait()
    matrices(weights, offsets, flat, tall, mats)
    for load in loads[2:]:
        load.wait()

    side = jnp.where(gy == 0, 0, 1)

    hand_on(hands_east, EAST)

    @pl.when(edge)
    def _():
        own_strip.wait()
        for r in tower:
            one_wait(r).wait_recv()
        for r in (*plane, None):
            target = gx if r is None else peers[r][0]
            block = owner[side, target]
            before, after = (block + 63) & 63, (block + 1) & 63
            column = gx & 51
            pick = jnp.where((before & 51) == column, before, jnp.where((after & 51) == column, after, block))
            part = gathered[(pick >> 2) & 3, :, 0:PAIRS, :]
            if r is None:
                landed[y, x, :, 0:PAIRS, :] = part
            else:
                chosen[r - PLANE, :, 0:PAIRS, :] = part
            if r is not None:

                @pl.when(later[r])
                def _():
                    pl.semaphore_wait(ready.at[r], 1)

                two_copy(r).start()

    remap((1, 2, 3, 4, 5, 6), GROUPS[:1], field, mats, out)

    hand_on(hands_west, WEST)
    start_later(sides, far)
    start_later(rows, far)

    for r in sides:
        side_copy(r).wait_recv()
    remap((1, 2, 3, 4, 5, 6), GROUPS[1:], field, mats, out)

    @pl.when(gy > 0)
    def _():
        for r in range(UP, DOWN):
            row_copy(r).wait_recv()
        remap((0,), GROUPS, field, mats, out)

    @pl.when(gy < 3)
    def _():
        for r in range(DOWN, ALONG_Z):
            row_copy(r).wait_recv()
        remap((7,), GROUPS, field, mats, out)

    @pl.when(edge)
    def _():
        for r in plane:
            two_wait(r).wait_recv()
        block = owner[side, gx]
        code = codes[side, gx]
        turn, flip = code & 1, (code >> 1) & 1
        before, after = (block + 63) & 63, (block + 1) & 63
        first, last = jnp.where(turn == 1, after, before), jnp.where(turn == 1, before, after)
        for u in range(EXT):
            if u < HALO:
                part, v = first, jnp.where(turn == 1, HALO - 1 - u, COLS - HALO + u)
            elif u < HALO + COLS:
                part, v = block, jnp.where(turn == 1, EXT - HALO - 1 - u, u - HALO)
            else:
                part, v = last, jnp.where(turn == 1, COLS - HALO + EXT - 1 - u, u - HALO - COLS)
            piece = landed[part >> 4, part & 3, v, 0:PAIRS, :]
            back = jnp.concatenate([piece[4:6], piece[2:4], piece[0:2]], axis=0)
            piece = jnp.where(flip == 1, back, piece)

            @pl.when(gy == 0)
            def _():
                field[u, 0:PAIRS, :] = piece

            @pl.when(gy == 3)
            def _():
                field[u, TOP : TOP + PAIRS, :] = piece

        remap((jnp.where(gy == 0, 0, BANDS - 1),), GROUPS, field, mats, out)
        for r in tower:
            one_copy(r).wait_send()
        for r in plane:
            two_copy(r).wait_send()

    for r, skip in ((WEST, via_to_west), (EAST, via_to_east)):

        @pl.when(jnp.logical_not(skip))
        def _():
            side_copy(r).wait_send()

    @pl.when(via_to_west | via_to_east)
    def _():
        for c in range(HALO):
            via_copy(WEST, c, c).wait_send()

    @pl.when(via_to_west & later[VIA])
    def _():
        pl.semaphore_wait(ready.at[VIA], 1)

    hand_wait(hands_west, WEST)
    hand_wait(hands_east, EAST)

    @pl.when(gy < 3)
    def _():
        for r in range(UP, DOWN):
            row_copy(r).wait_send()

    @pl.when(gy > 0)
    def _():
        for r in range(DOWN, ALONG_Z):
            row_copy(r).wait_send()


def on_device(tracers, weights, offsets, owner, codes):
    lines = tracers.reshape(COLS, LINES, 128)
    hbm = pl.BlockSpec(memory_space=pltpu.HBM)
    vmem = pl.BlockSpec(memory_space=pltpu.VMEM)
    dma = pltpu.SemaphoreType.DMA
    result = pl.pallas_call(
        kernel,
        out_shape=jax.ShapeDtypeStruct((COLS, LINES, 128), F32),
        in_specs=[hbm] * 5,
        out_specs=vmem,
        scratch_shapes=[
            pltpu.SMEM((2, 64), jnp.int32),
            pltpu.SMEM((2, 64), jnp.int32),
            pltpu.VMEM((EXT, TALL, 128), F32),
            pltpu.VMEM((COLS, 48, ROWS), F32),
            pltpu.VMEM((COLS, 4, ROWS), jnp.int32),
            pltpu.VMEM((24, 128 * COLS), F32),
            pltpu.VMEM((COLS, 256, 128), F32),
            pltpu.VMEM((2, BANDS, 8 * COLS, 256), F32),
            pltpu.VMEM((4, COLS, 8, 128), F32),
            pltpu.VMEM((15, COLS, 8, 128), F32),
            pltpu.VMEM((4, 4, COLS, 8, 128), F32),
            pltpu.VMEM((HALO, LINES, 128), F32),
            dma((6,)), dma((2,)), dma((2,)), dma((6,)), dma((6,)), dma((3,)), dma((4,)), dma((15,)), dma((4, 4)), dma((3,)), dma((3,)), dma((3,)), pltpu.SemaphoreType.REGULAR((LINKS,)),
        ],
        compiler_params=pltpu.CompilerParams(
            collective_id=0, has_side_effects=True, vmem_limit_bytes=40 * 1024 * 1024
        ),
    )(*(pltpu.with_memory_space_constraint(a, pltpu.HBM) for a in (owner, codes, lines, jnp.transpose(weights, (0, 2, 1)), jnp.transpose(offsets, (0, 2, 1)))))
    return result.reshape(COLS, ROWS, 2, 128)


def solution(mesh):
    in_specs = (P("gx", "gy", None, None), P("gx", "gy", None), P("gx", "gy", None), P(), P())
    return jax.shard_map(
        on_device, mesh=mesh, in_specs=in_specs, out_specs=P("gx", "gy", None, None), check_vma=False
    )
```

```python
import functools

import jax
import jax.numpy as jnp
from jax import lax
from jax.experimental import pallas as pl
from jax.experimental.pallas import tpu as pltpu
from jax.sharding import PartitionSpec as P

MESH = pl.DeviceIdType.MESH
F32, BF16 = jnp.float32, jnp.bfloat16
COLS, ROWS, HALO = 12, 64, 3
EXT = COLS + 2 * HALO
PAIRS = 2 * HALO
LINES = 2 * ROWS
TOP = LINES + PAIRS
TALL = 144
BANDS = 8
GROUPS = ((3, 6), (0, 3), (9, 3))


def stencil():
    shape = (32, 24)
    tap, term = (lax.broadcasted_iota(jnp.int32, shape, dim) for dim in range(2))
    piece, kind = term // 6, term % 6
    u, v = tap // 8 - piece // 2 - 1, tap % 8 - piece % 2 - 1
    near_u, near_v = jnp.abs(u) <= 1, jnp.abs(v) <= 1
    on_u, on_v = near_u & (v == 0), near_v & (u == 0)
    uf, vf = u.astype(F32), v.astype(F32)
    zero = jnp.zeros(shape, F32)
    centre = jnp.where((u == 0) & (v == 0), 1.0, zero)
    value = jnp.where(kind == 0, centre, zero)
    value = jnp.where((kind == 1) & on_u, 0.5 * uf, value)
    value = jnp.where((kind == 2) & on_v, 0.5 * vf, value)
    value = jnp.where((kind == 3) & on_u, 0.5 - 1.5 * centre, value)
    value = jnp.where((kind == 4) & on_v, 0.5 - 1.5 * centre, value)
    return jnp.where((kind == 5) & near_u & near_v, 0.25 * uf * vf, value)


def halves(value):
    high = value.astype(BF16)
    return high, (value - high.astype(F32)).astype(BF16)


def matrices(weights, offsets, flat, tall, mats):
    for x in range(COLS):
        w = weights[x]
        flat[:, 128 * x : 128 * x + 128] = jnp.concatenate([w[:24], w[24:]], axis=1)
    tall[...] = jnp.zeros_like(tall)
    coefs = jnp.dot(stencil(), flat[...], precision=lax.Precision.HIGHEST, preferred_element_type=F32)
    row = lax.broadcasted_iota(jnp.int32, (8, 128), 0)
    inner = lax.broadcasted_iota(jnp.int32, (8, 128), 1) % 8
    for first, count in GROUPS:
        for xl in range(count):
            x = first + xl
            o = offsets[x]
            cols = jnp.concatenate([o[0:1], o[2:3]], axis=1) + 2
            lines = jnp.concatenate([o[1:2], o[3:4]], axis=1) + 2
            shift = jnp.broadcast_to(lines, (8, 128)) + inner
            steps = jnp.broadcast_to(cols, (8, 128))
            pick = (row - shift) & 7
            in_low = row >= shift
            in_high = (row < shift) & (shift <= row + 8)
            zero = jnp.zeros((8, 128), F32)
            low, high = [], []
            for i in range(4):
                turned = jnp.take_along_axis(coefs[8 * i : 8 * i + 8, 128 * x : 128 * x + 128], pick, axis=0)
                low.append(jnp.where(in_low, turned, zero))
                high.append(jnp.where(in_high, turned, zero))
            odd, two = (steps & 1) == 1, steps >= 2
            for part, pieces in enumerate((low, high)):
                pieces = [zero] + pieces + [zero]
                once = [jnp.where(odd, pieces[d], pieces[d + 1]) for d in range(5)]
                once = [zero, zero] + once + [zero, zero]
                for d in range(7):
                    at = 16 * (xl + d) + 8 * part
                    tall[x, at : at + 8, :] = jnp.where(two, once[d], once[d + 2])
    for x in range(COLS):
        mats[:, :, 8 * x : 8 * x + 8, :] = jnp.transpose(tall[x]).reshape(2, BANDS, 8, 256)


def remap(bands, groups, field, mats, out):
    for b in bands:
        base = 16 * b if isinstance(b, int) else pl.multiple_of(16 * b, 16)
        for first, count in groups:
            depth = 16 * (count + PAIRS)
            for level in range(2):
                mat = mats[level, b, 8 * first : 8 * (first + count), :depth]
                mat_high, mat_low = halves(mat)
                cells = field[first : first + count + PAIRS, pl.ds(base + level, 16, 2), :]
                cell_high, cell_low = halves(cells.reshape(depth, 128))
                both = jnp.dot(mat_high, jnp.concatenate([cell_high, cell_low], axis=1), preferred_element_type=F32)
                result = both[:, :128] + both[:, 128:] + jnp.dot(mat_low, cell_high, preferred_element_type=F32)
                for xl in range(count):
                    out[first + xl, pl.ds(base + level, 8, 2), :] = result[8 * xl : 8 * xl + 8]


WEST, EAST, UP, DOWN, ALONG_Z, PLANE = 0, 1, 2, 5, 8, 11
VIA, LINKS = 26, 27
ORDER = (*range(ALONG_Z, LINKS), *range(ALONG_Z))
STEPS = sorted(((j, i) for j in range(4) for i in range(4) if j + i), key=lambda s: (-(0, 1, 2, 1)[s[1]], -(0, 1, 2, 1)[s[0]]))
BACK = (1, 0, 5, 7, 6, 2, 4, 3) + (10, 9, 8) + tuple(
    PLANE + STEPS.index((-j % 4, -i % 4)) for j, i in STEPS
) + (VIA,)


def rank(gx, gy):
    return (gy >> 1) * 256 + ((gx & 15) << 3) + ((gx >> 4) << 1) + 1 - (gy & 1)


def kernel(
    owner_in, codes_in, tracers, weights_in, offsets_in, out,
    owner, codes, field, weights, offsets, flat, tall, mats, gathered, chosen, landed, relay,
    in_sem, side_send, side_recv, row_send, row_recv, one_send, one_recv, two_send, two_recv,
    via_send, via_recv, hand_send, ready,
):
    gx, gy = lax.axis_index("gx"), lax.axis_index("gy")
    y, z, x = gx >> 4, (gx >> 2) & 3, gx & 3
    east, west = (gx + 1) & 63, (gx + 63) & 63
    edge = (gy == 0) | (gy == 3)
    half = COLS // 2
    edge_at = jnp.where(gy == 0, 0, LINES - PAIRS)

    loads = [
        pltpu.make_async_copy(weights_in, weights, in_sem.at[0]),
        pltpu.make_async_copy(offsets_in, offsets, in_sem.at[1]),
        pltpu.make_async_copy(owner_in, owner, in_sem.at[4]),
        pltpu.make_async_copy(codes_in, codes, in_sem.at[5]),
        pltpu.make_async_copy(tracers, field.at[HALO : HALO + COLS, PAIRS:TOP, :], in_sem.at[2]),
    ]
    own_strip = pltpu.make_async_copy(
        tracers.at[:, pl.ds(edge_at, PAIRS), :], gathered.at[z, :, 0:PAIRS, :], in_sem.at[3]
    )

    always = gy >= 0
    peers = [(west, gy), (east, gy)]
    exists = [always, always]
    for to, there in ((gy + 1, gy < 3), (gy - 1, gy > 0)):
        peers += [(gx, to), (west, to), (east, to)]
        exists += [there] * 3
    peers += [(16 * y + 4 * ((z + k) & 3) + x, gy) for k in (1, 2, 3)]
    peers += [(16 * ((y + j) & 3) + 4 * z + ((x + i) & 3), gy) for j, i in STEPS]
    exists += [edge] * 18
    wraps_west, wraps_east = (z == 0) & (x == 0), (z == 3) & (x == 3)
    hands_west, hands_east = edge & (z == 0) & (x == 1), edge & (z == 3) & (x == 2)
    via_to_east, via_to_west = edge & wraps_east, edge & wraps_west
    up_y, down_y = 16 * ((y + 1) & 3), 16 * ((y + 3) & 3)
    via = jnp.where(
        via_to_east, up_y + 1, jnp.where(hands_west, down_y + 15, jnp.where(via_to_west, down_y + 14, up_y))
    )
    peers += [(via, gy)]
    exists += [via_to_east | via_to_west | hands_west | hands_east]
    exists[WEST] = jnp.logical_not(via_to_west)
    exists[EAST] = jnp.logical_not(via_to_east)
    mine = rank(gx, gy)
    later = [there & (rank(*to) > mine) for to, there in zip(peers, exists)]
    earlier = [there & (rank(*to) < mine) for to, there in zip(peers, exists)]

    barrier = pltpu.get_barrier_semaphore()
    for r in ORDER:

        @pl.when(later[r])
        def _():
            pl.semaphore_signal(barrier, inc=1, device_id=peers[r], device_id_type=MESH)

    @pl.when(edge)
    def _():
        own_strip.start()

    for load in loads:
        load.start()

    ahead = sum(e.astype(jnp.int32) for e in earlier)

    @pl.when(ahead > 0)
    def _():
        pl.semaphore_wait(barrier, ahead)

    def send(source, target, send_sem, recv_sem, to):
        return pltpu.make_async_remote_copy(
            src_ref=source, dst_ref=target, send_sem=send_sem, recv_sem=recv_sem, device_id=to, device_id_type=MESH
        )

    def side_copy(r):
        if r == WEST:
            source, target = tracers.at[0:HALO], field.at[HALO + COLS : EXT, PAIRS:TOP, :]
        else:
            source, target = tracers.at[COLS - HALO : COLS], field.at[0:HALO, PAIRS:TOP, :]
        return send(source, target, side_send.at[r], side_recv.at[r], peers[r])

    def row_copy(r):
        up = r < DOWN
        lines = pl.ds(LINES - PAIRS, PAIRS) if up else pl.ds(0, PAIRS)
        target = pl.ds(0, PAIRS) if up else pl.ds(TOP, PAIRS)
        which = (r - UP) % 3
        taken, put = (
            (slice(0, COLS), slice(HALO, HALO + COLS)),
            (slice(0, HALO), slice(HALO + COLS, EXT)),
            (slice(COLS - HALO, COLS), slice(0, HALO)),
        )[which]
        return send(
            tracers.at[taken, lines, :], field.at[put, target, :], row_send.at[r - UP], row_recv.at[r - UP], peers[r]
        )

    def one_copy(r):
        k = r - ALONG_Z
        return send(
            tracers.at[:, pl.ds(edge_at, PAIRS), :], gathered.at[z, :, 0:PAIRS, :], one_send.at[k], one_recv.at[z], peers[r]
        )

    def one_wait(r):
        k = r - ALONG_Z
        spot = (z + k + 1) & 3
        place = gathered.at[spot, :, 0:PAIRS, :]
        return send(place, place, one_send.at[k], one_recv.at[spot], peers[r])

    def two_copy(r):
        k = r - PLANE
        return send(
            chosen.at[k, :, 0:PAIRS, :], landed.at[y, x, :, 0:PAIRS, :], two_send.at[k], two_recv.at[y, x], peers[r]
        )

    def two_wait(r):
        k = r - PLANE
        j, i = STEPS[k]
        there = (y + j) & 3, (x + i) & 3
        return send(
            chosen.at[k, :, 0:PAIRS, :], landed.at[*there, :, 0:PAIRS, :], two_send.at[k], two_recv.at[*there], peers[r]
        )

    def copy_of(r):
        return side_copy(r) if r < UP else row_copy(r) if r < ALONG_Z else one_copy(r)

    def start_earlier(links):
        for r in links:

            @pl.when(earlier[r])
            def _():
                copy_of(r).start()

    def start_later(links, allowed):
        for r in links:

            @pl.when(later[r] & allowed(r))
            def _():
                pl.semaphore_wait(ready.at[r], 1)
                copy_of(r).start()

    def far(r):
        wrap = wraps_west if r in (WEST, UP + 1, DOWN + 1) else wraps_east if r in (EAST, UP + 2, DOWN + 2) else gy < 0
        return wrap | ((gy == 1) if UP <= r < DOWN else (gy == 2) if DOWN <= r < ALONG_Z else gy < 0)

    def near(r):
        return jnp.logical_not(far(r))

    def via_copy(r, c, column):
        return send(tracers.at[column], relay.at[c], via_send.at[c], via_recv.at[c], peers[r])

    def start_via(allowed, r, first):
        @pl.when(allowed)
        def _():
            for c in range(HALO):
                via_copy(r, c, first + c).start()

    def hand_copy(r, c):
        column = c if r == EAST else HALO + COLS + c
        return send(relay.at[c], field.at[column, PAIRS:TOP, :], hand_send.at[c], side_recv.at[r], peers[VIA])

    def hand_on(allowed, r):
        @pl.when(allowed & later[VIA])
        def _():
            pl.semaphore_wait(ready.at[VIA], 1)

        @pl.when(allowed)
        def _():
            for c in range(HALO):
                via_copy(r, c, c).wait_recv()
                hand_copy(r, c).start()

    def hand_wait(allowed, r):
        @pl.when(allowed)
        def _():
            for c in range(HALO):
                hand_copy(r, c).wait_send()

    rows, sides, plane = range(UP, ALONG_Z), (WEST, EAST), range(PLANE, VIA)
    tower = range(ALONG_Z, PLANE)
    not_edge = jnp.logical_not(edge)

    def start_sides(who):
        for r in sides:

            @pl.when(who & earlier[r])
            def _():
                copy_of(r).start()

        start_later(sides, lambda r: who & near(r))

    start_earlier(tower)
    for r in ORDER:

        @pl.when(earlier[r])
        def _():
            pl.semaphore_signal(ready.at[BACK[r]], inc=1, device_id=peers[r], device_id_type=MESH)

    start_earlier(rows)
    start_sides(not_edge)
    start_via(via_to_east, WEST, COLS - HALO)
    start_later(rows, lambda r: near(r) & not_edge)
    start_later(tower, lambda r: always)
    start_sides(edge)
    start_via(via_to_west, EAST, 0)
    start_later(rows, lambda r: near(r) & edge)

    for c in range(EXT):
        field[c, TOP + PAIRS : TALL, :] = jnp.zeros((TALL - TOP - PAIRS, 128), F32)

    loads[0].wait()
    loads[1].wait()
    matrices(weights, offsets, flat, tall, mats)
    for load in loads[2:]:
        load.wait()

    side = jnp.where(gy == 0, 0, 1)

    hand_on(hands_east, EAST)

    @pl.when(edge)
    def _():
        own_strip.wait()
        for r in tower:
            one_wait(r).wait_recv()
        for r in (*plane, None):
            target = gx if r is None else peers[r][0]
            block = owner[side, target]
            before, after = (block + 63) & 63, (block + 1) & 63
            column = gx & 51
            pick = jnp.where((before & 51) == column, before, jnp.where((after & 51) == column, after, block))
            part = gathered[(pick >> 2) & 3, :, 0:PAIRS, :]
            if r is None:
                landed[y, x, :, 0:PAIRS, :] = part
            else:
                chosen[r - PLANE, :, 0:PAIRS, :] = part
            if r is not None:

                @pl.when(later[r])
                def _():
                    pl.semaphore_wait(ready.at[r], 1)

                two_copy(r).start()

    remap((1, 2, 3, 4, 5, 6), GROUPS[:1], field, mats, out)

    hand_on(hands_west, WEST)
    start_later(sides, far)
    start_later(rows, far)

    for r in sides:
        side_copy(r).wait_recv()
    remap((1, 2, 3, 4, 5, 6), GROUPS[1:], field, mats, out)

    @pl.when(gy > 0)
    def _():
        for r in range(UP, DOWN):
            row_copy(r).wait_recv()
        remap((0,), GROUPS, field, mats, out)

    @pl.when(gy < 3)
    def _():
        for r in range(DOWN, ALONG_Z):
            row_copy(r).wait_recv()
        remap((7,), GROUPS, field, mats, out)

    @pl.when(edge)
    def _():
        for r in plane:
            two_wait(r).wait_recv()
        block = owner[side, gx]
        code = codes[side, gx]
        turn, flip = code & 1, (code >> 1) & 1
        before, after = (block + 63) & 63, (block + 1) & 63
        first, last = jnp.where(turn == 1, after, before), jnp.where(turn == 1, before, after)
        for u in range(EXT):
            if u < HALO:
                part, v = first, jnp.where(turn == 1, HALO - 1 - u, COLS - HALO + u)
            elif u < HALO + COLS:
                part, v = block, jnp.where(turn == 1, EXT - HALO - 1 - u, u - HALO)
            else:
                part, v = last, jnp.where(turn == 1, COLS - HALO + EXT - 1 - u, u - HALO - COLS)
            piece = landed[part >> 4, part & 3, v, 0:PAIRS, :]
            back = jnp.concatenate([piece[4:6], piece[2:4], piece[0:2]], axis=0)
            piece = jnp.where(flip == 1, back, piece)

            @pl.when(gy == 0)
            def _():
                field[u, 0:PAIRS, :] = piece

            @pl.when(gy == 3)
            def _():
                field[u, TOP : TOP + PAIRS, :] = piece

        remap((jnp.where(gy == 0, 0, BANDS - 1),), GROUPS, field, mats, out)
        for r in tower:
            one_copy(r).wait_send()
        for r in plane:
            two_copy(r).wait_send()

    for r, skip in ((WEST, via_to_west), (EAST, via_to_east)):

        @pl.when(jnp.logical_not(skip))
        def _():
            side_copy(r).wait_send()

    @pl.when(via_to_west | via_to_east)
    def _():
        for c in range(HALO):
            via_copy(WEST, c, c).wait_send()

    @pl.when(via_to_west & later[VIA])
    def _():
        pl.semaphore_wait(ready.at[VIA], 1)

    hand_wait(hands_west, WEST)
    hand_wait(hands_east, EAST)

    @pl.when(gy < 3)
    def _():
        for r in range(UP, DOWN):
            row_copy(r).wait_send()

    @pl.when(gy > 0)
    def _():
        for r in range(DOWN, ALONG_Z):
            row_copy(r).wait_send()


def on_device(tracers, weights, offsets, owner, codes):
    lines = tracers.reshape(COLS, LINES, 128)
    hbm = pl.BlockSpec(memory_space=pltpu.HBM)
    vmem = pl.BlockSpec(memory_space=pltpu.VMEM)
    dma = pltpu.SemaphoreType.DMA
    result = pl.pallas_call(
        kernel,
        out_shape=jax.ShapeDtypeStruct((COLS, LINES, 128), F32),
        in_specs=[hbm] * 5,
        out_specs=vmem,
        scratch_shapes=[
            pltpu.SMEM((2, 64), jnp.int32),
            pltpu.SMEM((2, 64), jnp.int32),
            pltpu.VMEM((EXT, TALL, 128), F32),
            pltpu.VMEM((COLS, 48, ROWS), F32),
            pltpu.VMEM((COLS, 4, ROWS), jnp.int32),
            pltpu.VMEM((24, 128 * COLS), F32),
            pltpu.VMEM((COLS, 256, 128), F32),
            pltpu.VMEM((2, BANDS, 8 * COLS, 256), F32),
            pltpu.VMEM((4, COLS, 8, 128), F32),
            pltpu.VMEM((15, COLS, 8, 128), F32),
            pltpu.VMEM((4, 4, COLS, 8, 128), F32),
            pltpu.VMEM((HALO, LINES, 128), F32),
            dma((6,)), dma((2,)), dma((2,)), dma((6,)), dma((6,)), dma((3,)), dma((4,)), dma((15,)), dma((4, 4)), dma((3,)), dma((3,)), dma((3,)), pltpu.SemaphoreType.REGULAR((LINKS,)),
        ],
        compiler_params=pltpu.CompilerParams(
            collective_id=0, has_side_effects=True, vmem_limit_bytes=40 * 1024 * 1024
        ),
    )(*(pltpu.with_memory_space_constraint(a, pltpu.HBM) for a in (owner, codes, lines, jnp.transpose(weights, (0, 2, 1)), jnp.transpose(offsets, (0, 2, 1)))))
    return result.reshape(COLS, ROWS, 2, 128)


def solution(mesh):
    in_specs = (P("gx", "gy", None, None), P("gx", "gy", None), P("gx", "gy", None), P(), P())
    return jax.shard_map(
        on_device, mesh=mesh, in_specs=in_specs, out_specs=P("gx", "gy", None, None), check_vma=False
    )
```
